256 devices in a mesh: rep: 32 (over z_lo, x, y), fsdp: 8 (over z_hi, core).
Axes of the slice: x: 4, y: 4, z: 8 (z_hi: 4, z_lo: 2; z = z_hi * 2 + z_lo), core: 2. Of those that a mesh axis runs over, the one named last changes fastest.
Arguments:
- activations: bfloat16 [180224, 4096], P(('rep', 'fsdp')), may hold values from -6 to 6
- cotangent: bfloat16 [180224, 512], P(('rep', 'fsdp')), may hold values from -0.078125 to 0.078125
- master: float32 [32, 4096, 512], P('rep', 'fsdp'), may hold values from -6 to 6
- moment_one: float32 [32, 4096, 512], P('rep', 'fsdp'), may hold values from -4 to 4
- moment_two: float32 [32, 4096, 512], P('rep', 'fsdp'), may hold values from 0.01 to 1
- push_weight: float32 [32], P('rep'), may hold values from 0.5 to 2
- step_index: int32 [1], replicated, may hold values from 0 to 999
Outputs:
- master_new: float32 [32, 4096, 512], P('rep', 'fsdp')
- moment_one_new: float32 [32, 4096, 512], P('rep', 'fsdp')
- moment_two_new: float32 [32, 4096, 512], P('rep', 'fsdp')
- weight_new: float32 [32], P('rep')
- params_copy: bfloat16 [32, 4096, 512], P('rep', 'fsdp')
The draws below stay inside these ranges and needn't reach their ends.
All inputs are finite; a program needn't handle non-finite values.
Results may differ from the reference program's by a relative error of at most 0.01.
Values may be sent and summed in bfloat16 or wider, within the bound.
No kernel may reach another device: no remote copies, remote signals or barrier semaphores. Data moves between devices by JAX's collectives and lax.ppermute only.
A program may use at most 128 MiB of HBM per device.

```python
import math
import jax
import jax.numpy as jnp
from jax import lax

D = 4096
KVW = 512
TOK_DEV = 704
REPLICAS = 32
ROWS = 180224
N_REP = 32
N_FSDP = 8


def block_levels(rng, extent, pieces, low, top_value):
    gain, own = 1.0, jax.random.fold_in(rng, 6)
    for axis_at, shards_of in pieces:
        steps = jnp.exp(jax.random.uniform(jax.random.fold_in(own, axis_at), (shards_of,), jnp.float32, low / len(pieces), top_value / len(pieces)))
        gain = gain * jnp.repeat(steps, extent[axis_at] // shards_of).reshape([-1 if axis == axis_at else 1 for axis in range(len(extent))])
    return gain


def normal_values(stream_key, extent, deviation, limit, shards=(), held_as=jnp.bfloat16):
    gain = block_levels(stream_key, extent, shards, -0.22, 0.18) if shards else 1.0
    values = jax.random.normal(stream_key, extent, jnp.float32) * deviation * gain
    return jnp.minimum(jnp.maximum(values, -limit), limit).astype(held_as)


def setup_inputs(seed: int = 0) -> dict:
    splits = jax.random.split(jax.random.key(seed), 8)
    return {
        "activations": normal_values(splits[0], (ROWS, D), 1.0, 6.0, ((0, 256),)),
        "cotangent": normal_values(splits[1], (ROWS, KVW), (TOK_DEV * N_FSDP) ** -0.5, 0.078125, ((0, 256),)),
        "master": normal_values(splits[2], (REPLICAS, D, KVW), 1.0, 6.0, ((0, 32), (1, 8)), jnp.float32),
        "moment_one": normal_values(splits[3], (REPLICAS, D, KVW), 0.5, 4.0, ((0, 32), (1, 8)), jnp.float32),
        "moment_two": jnp.clip(jnp.exp(math.log(1.0) - 4.6051702 * jax.random.uniform(splits[4], (REPLICAS, D, KVW), jnp.float32) ** block_levels(splits[4], (REPLICAS, D, KVW), ((0, 32), (1, 8)), -0.2, 0.2)), 0.01, 1.0),
        "push_weight": jnp.clip(jnp.exp(math.log(2.0) - 1.3862944 * jax.random.uniform(splits[5], (REPLICAS,), jnp.float32) ** block_levels(splits[5], (REPLICAS,), ((0, 32),), -0.2, 0.2)), 0.5, 2.0),
        "step_index": jax.random.randint(splits[6], (1,), 0, 1000).astype(jnp.int32),
    }


BETA_ONE = 0.9
BETA_TWO = 0.95
LEARN_RATE = 0.01
DECAY_RATE = 0.1
EPSILON = 1e-08

def replica_gradient(blocks):
    inputs, grads_out = blocks
    return lax.dot_general(inputs, grads_out, (((0,), (0,)), ((), ())), preferred_element_type=jnp.float32)

def reference(activations, cotangent, master, moment_one, moment_two, push_weight, step_index):
    replicas = N_REP
    row_count = activations.shape[0] // replicas
    inputs = activations.reshape(replicas, row_count, D)
    grads_out = cotangent.reshape(replicas, row_count, KVW)
    gradient = lax.map(replica_gradient, (inputs, grads_out))
    counter = step_index[0]
    steps_done = (counter + 1).astype(jnp.float32)
    first = BETA_ONE * moment_one + (1.0 - BETA_ONE) * gradient
    second = BETA_TWO * moment_two + (1.0 - BETA_TWO) * gradient * gradient
    corr_one = 1.0 - jnp.power(jnp.float32(BETA_ONE), steps_done)
    corr_two = 1.0 - jnp.power(jnp.float32(BETA_TWO), steps_done)
    direction = first / corr_one / (jnp.sqrt(second / corr_two) + EPSILON)
    weights = push_weight[:, None, None]
    halfway = master - LEARN_RATE * (direction + DECAY_RATE * master / weights)
    bit_count = replicas.bit_length() - 1
    offset = counter % bit_count
    indices = jnp.arange(replicas, dtype=jnp.int32)
    partner = jnp.bitwise_xor(indices, jnp.left_shift(jnp.int32(1), offset.astype(jnp.int32)))
    master_new = 0.5 * (halfway + halfway[partner])
    first_new = 0.5 * (first + first[partner])
    weight_new = 0.5 * (push_weight + push_weight[partner])
    params_copy = (master_new / weight_new[:, None, None]).astype(jnp.bfloat16)
    return (master_new, first_new, second, weight_new, params_copy)
```

```python
from functools import partial

import jax
import jax.numpy as jnp
from jax import lax
from jax.experimental import pallas as pl
from jax.experimental.pallas import tpu as pltpu
from jax.sharding import PartitionSpec as P

BETA_ONE = 0.9
BETA_TWO = 0.95
LEARN_RATE = 0.01
DECAY_RATE = 0.1
EPSILON = 1e-08

F32 = jnp.float32
BF16 = jnp.bfloat16
ANY = pl.BlockSpec(memory_space=pl.ANY)
SMEM = pl.BlockSpec(memory_space=pltpu.SMEM)
VMEM_LIMIT = 48 * 1024 * 1024
CHUNKS = ((0, 256), (256, 256))


def params(**more):
    return pltpu.CompilerParams(vmem_limit_bytes=VMEM_LIMIT, **more)


def product(x, g):
    return lax.dot_general(x, g, (((0,), (0,)), ((), ())), preferred_element_type=F32)


def cost(blocks, tokens, width, columns):
    return pl.CostEstimate(
        flops=2 * blocks * tokens * width * columns,
        bytes_accessed=blocks * (tokens * width * 2 + width * columns * 2),
        transcendentals=0,
    )


def other_kernel(at, x, g, out):
    out[...] = product(x[...], g[...]).astype(BF16)


def other_blocks(places, x, g, width):
    tokens, columns = g.shape
    count = places.shape[0]
    return pl.pallas_call(
        other_kernel,
        grid_spec=pltpu.PrefetchScalarGridSpec(
            num_scalar_prefetch=1,
            grid=(count,),
            in_specs=[
                pl.BlockSpec((tokens, width), lambda i, at: (0, at[i])),
                pl.BlockSpec((tokens, columns), lambda i, at: (0, 0)),
            ],
            out_specs=pl.BlockSpec((width, columns), lambda i, at: (i, 0)),
        ),
        out_shape=jax.ShapeDtypeStruct((count * width, columns), BF16),
        compiler_params=params(),
        cost_estimate=cost(count, tokens, width, columns),
        name="other_blocks",
    )(places, x, g)


def far_kernel(at, x, g, got, *outs):
    total = product(x[...], g[...]) + got[...].astype(F32)
    for k, (low, rows) in enumerate(CHUNKS):
        half = rows // 2
        outs[2 * k][...] = total[low : low + half].astype(BF16)
        outs[2 * k + 1][...] = total[low + half : low + rows].astype(BF16)


def far_block(place, x, g, got, width):
    tokens, columns = g.shape
    shapes = []
    for low, rows in CHUNKS:
        shapes += [jax.ShapeDtypeStruct((rows // 2, columns), BF16)] * 2
    return pl.pallas_call(
        far_kernel,
        grid_spec=pltpu.PrefetchScalarGridSpec(
            num_scalar_prefetch=1,
            grid=(1,),
            in_specs=[
                pl.BlockSpec((tokens, width), lambda i, at: (0, at[0])),
                pl.BlockSpec((tokens, columns), lambda i, at: (0, 0)),
                pl.BlockSpec((width, columns), lambda i, at: (0, 0)),
            ],
            out_specs=[pl.BlockSpec(s.shape, lambda i, at: (0, 0)) for s in shapes],
        ),
        out_shape=shapes,
        compiler_params=params(),
        cost_estimate=cost(1, tokens, width, columns),
        name="far_block",
    )(place, x, g, got)


def near_kernel(at, x, g, got, *outs):
    total = product(x[...], g[...]) + got[...].astype(F32)
    count = len(CHUNKS)

    @pl.when(pl.program_id(0) == 0)
    def _():
        for k, (low, rows) in enumerate(CHUNKS):
            half = rows // 2
            outs[k][...] = total[low : low + half]
            outs[count + k][...] = total[low + half : low + rows].astype(BF16)

    @pl.when(pl.program_id(0) == 1)
    def _():
        for k, (low, rows) in enumerate(CHUNKS):
            half = rows // 2
            outs[2 * count + k][...] = total[low + half : low + rows]
            outs[3 * count + k][...] = total[low : low + half].astype(BF16)


def near_blocks(places, x, g, got, width):
    tokens, columns = g.shape
    shapes = []
    for dtype in (F32, BF16, F32, BF16):
        shapes += [jax.ShapeDtypeStruct((rows // 2, columns), dtype) for _, rows in CHUNKS]
    outs = pl.pallas_call(
        near_kernel,
        grid_spec=pltpu.PrefetchScalarGridSpec(
            num_scalar_prefetch=1,
            grid=(2,),
            in_specs=[
                pl.BlockSpec((tokens, width), lambda i, at: (0, at[i])),
                pl.BlockSpec((tokens, columns), lambda i, at: (0, 0)),
                pl.BlockSpec((width, columns), lambda i, at: (i, 0)),
            ],
            out_specs=[pl.BlockSpec(s.shape, lambda i, at: (0, 0)) for s in shapes],
        ),
        out_shape=shapes,
        compiler_params=params(),
        cost_estimate=cost(2, tokens, width, columns),
        name="near_blocks",
    )(places, x, g, got)
    count = len(CHUNKS)
    return [outs[i * count : (i + 1) * count] for i in range(4)]


def own_kernel(at, x, g, got, out):
    out[...] = product(x[...], g[...]) + got[...].astype(F32)


def own_block(place, x, g, got, width):
    tokens, columns = g.shape
    return pl.pallas_call(
        own_kernel,
        grid_spec=pltpu.PrefetchScalarGridSpec(
            num_scalar_prefetch=1,
            grid=(1,),
            in_specs=[
                pl.BlockSpec((tokens, width), lambda i, at: (0, at[0])),
                pl.BlockSpec((tokens, columns), lambda i, at: (0, 0)),
                pl.BlockSpec((width, columns), lambda i, at: (2, 0)),
            ],
            out_specs=pl.BlockSpec((width, columns), lambda i, at: (0, 0)),
        ),
        out_shape=jax.ShapeDtypeStruct((width, columns), F32),
        compiler_params=params(),
        cost_estimate=cost(1, tokens, width, columns),
        name="own_block",
    )(place, x, g, got)


def add_kernel(up, far_up, down, far_down, out_up, out_down):
    out_up[...] = (up[...] + far_up[...].astype(F32)).astype(BF16)
    out_down[...] = (down[...] + far_down[...].astype(F32)).astype(BF16)


def add_far(up, far_up, down, far_down):
    return pl.pallas_call(
        add_kernel,
        out_shape=[jax.ShapeDtypeStruct(up.shape, BF16)] * 2,
        compiler_params=params(),
        cost_estimate=pl.CostEstimate(flops=2 * up.size, bytes_accessed=16 * up.size, transcendentals=0),
        name="add_far",
    )(up, far_up, down, far_down)


def step_kernel(half, scales, own, c_up, b_down, b_up, c_down, master, one, two, *rest):
    second_out, halfway_out, first_out, send = rest[-4:]
    rows = 2 * half
    for low, near, far in ((0, c_up, b_down), (half, b_up, c_down)):
        at = pl.ds(low, half)
        gradient = own[at] + (near[...].astype(F32) + far[...].astype(F32))
        first = BETA_ONE * one[at] + (1.0 - BETA_ONE) * gradient
        second = BETA_TWO * two[at] + (1.0 - BETA_TWO) * gradient * gradient
        direction = first * scales[0] / (jnp.sqrt(second * scales[1]) + EPSILON)
        weights = master[at]
        halfway = weights - LEARN_RATE * (direction + weights * scales[2])
        second_out[at] = second
        halfway_out[at] = halfway
        first_out[at] = first
        send[at] = halfway.astype(BF16)
        send[pl.ds(rows + low, half)] = first.astype(BF16)


def step_chunk(low, rows, scales, own, c_up, b_down, b_up, c_down, master, one, two, before):
    height, columns = master.shape
    half = rows // 2
    place = low // rows
    here = pl.BlockSpec((rows, columns), lambda i: (place, 0))
    whole = pl.BlockSpec((half, columns), lambda i: (0, 0))
    flat = pl.BlockSpec((rows, columns), lambda i: (0, 0))
    ins = [scales, own, c_up, b_down, b_up, c_down, master, one, two]
    specs = [SMEM, here, whole, whole, whole, whole, here, here, here]
    aliases = {}
    if before is not None:
        aliases = {len(ins): 0}
        ins.append(before)
        specs.append(ANY)
    return pl.pallas_call(
        partial(step_kernel, half),
        grid=(1,),
        in_specs=specs,
        out_specs=[here, flat, flat, pl.BlockSpec((2 * rows, columns), lambda i: (0, 0))],
        out_shape=[
            jax.ShapeDtypeStruct((height, columns), F32),
            jax.ShapeDtypeStruct((rows, columns), F32),
            jax.ShapeDtypeStruct((rows, columns), F32),
            jax.ShapeDtypeStruct((2 * rows, columns), BF16),
        ],
        input_output_aliases=aliases,
        compiler_params=params(),
        cost_estimate=pl.CostEstimate(
            flops=20 * rows * columns, bytes_accessed=40 * rows * columns, transcendentals=2 * rows * columns
        ),
        name="step_chunk",
    )(*ins)


def mix_kernel(rows, scales, halfway, first, got, *rest):
    master_out, first_out, copy_out = rest[-3:]
    mixed = 0.5 * (halfway[...] + got[0:rows].astype(F32))
    master_out[...] = mixed
    first_out[...] = 0.5 * (first[...] + got[rows : 2 * rows].astype(F32))
    copy_out[...] = (mixed * scales[0]).astype(BF16)


def mix_chunk(low, rows, scales, halfway, first, got, before, height):
    columns = halfway.shape[1]
    place = low // rows
    here = pl.BlockSpec((rows, columns), lambda i: (place, 0))
    flat = pl.BlockSpec((rows, columns), lambda i: (0, 0))
    ins = [scales, halfway, first, got]
    specs = [SMEM, flat, flat, pl.BlockSpec((2 * rows, columns), lambda i: (0, 0))]
    aliases = {}
    if before is not None:
        aliases = {len(ins) + i: i for i in range(3)}
        ins += list(before)
        specs += [ANY] * 3
    return pl.pallas_call(
        partial(mix_kernel, rows),
        grid=(1,),
        in_specs=specs,
        out_specs=[here] * 3,
        out_shape=[
            jax.ShapeDtypeStruct((height, columns), F32),
            jax.ShapeDtypeStruct((height, columns), F32),
            jax.ShapeDtypeStruct((height, columns), BF16),
        ],
        input_output_aliases=aliases,
        compiler_params=params(),
        cost_estimate=pl.CostEstimate(flops=5 * rows * columns, bytes_accessed=22 * rows * columns, transcendentals=0),
        name="mix_chunk",
    )(*ins)


def up_z(block):
    count = lax.axis_size("fsdp")
    return lax.ppermute(block, "fsdp", [(i, (i + 2) % count) for i in range(count)])


def down_z(block):
    count = lax.axis_size("fsdp")
    return lax.ppermute(block, "fsdp", [(i, (i - 2) % count) for i in range(count)])


def other_core(block):
    return lax.ppermute(block, "fsdp", [(i, i ^ 1) for i in range(lax.axis_size("fsdp"))])


def from_partner(block, bit):
    return lax.ppermute(block, "rep", [(i, i ^ (1 << bit)) for i in range(lax.axis_size("rep"))])


def after(value, *earlier):
    return lax.optimization_barrier((value, *earlier))[0]


def whole_step(bit, x, g, master, one, two, push_weight, scales):
    height, columns = master.shape
    me = lax.axis_index("fsdp")
    groups = lax.axis_size("fsdp") // 2
    group, core = me // 2, me % 2
    far, above, below = [(group + d) % groups for d in (2, 1, groups - 1)]

    def places(which, *at):
        return jnp.stack([2 * a + which for a in at]).astype(jnp.int32)

    theirs = 1 - core
    weight_new = 0.5 * (push_weight + from_partner(push_weight, bit))
    out_far = other_blocks(places(theirs, far), x, g, height)
    got_far = other_core(out_far)
    out_near = other_blocks(places(theirs, above, below, group), x, g, height)
    got_near = other_core(out_near)
    aways = far_block(places(core, far), x, g, got_far, height)
    c_ups, b_ups, c_downs, b_downs = near_blocks(places(core, above, below), x, g, got_near, height)
    own = own_block(places(core, group), x, g, got_near, height)

    second = mixed = None
    mix_scales = 1.0 / weight_new
    gates = []
    for k, (low, rows) in enumerate(CHUNKS):
        a_up, a_down = aways[2 * k], aways[2 * k + 1]
        b_up, b_down = b_ups[k], b_downs[k]
        if gates:
            a_up, a_down = after(a_up, gates[0]), after(a_down, gates[1])
            b_up, b_down = after(b_up, gates[2]), after(b_down, gates[3])
        got_a_up, got_a_down = up_z(a_up), down_z(a_down)
        got_b_up, got_b_down = up_z(b_up), down_z(b_down)
        c_up, c_down = add_far(c_ups[k], got_a_up, c_downs[k], got_a_down)
        got_c_up, got_c_down = up_z(c_up), down_z(c_down)
        gates = [got_b_up, got_b_down, got_c_up, got_c_down]
        second, halfway, first, send = step_chunk(
            low, rows, scales, own, got_c_up, got_b_down, got_b_up, got_c_down, master, one, two, second
        )
        got = from_partner(send, bit)
        mixed = mix_chunk(low, rows, mix_scales, halfway, first, got, mixed, height)
    return (mixed[0], mixed[1], second, weight_new, mixed[2])


def on_device(activations, cotangent, master, moment_one, moment_two, push_weight, step_index):
    counter = step_index[0]
    steps_done = (counter + 1).astype(F32)
    corr_one = 1.0 - jnp.power(F32(BETA_ONE), steps_done)
    corr_two = 1.0 - jnp.power(F32(BETA_TWO), steps_done)
    scales = jnp.stack([1.0 / corr_one, 1.0 / corr_two, DECAY_RATE / push_weight[0]])
    bits = lax.axis_size("rep").bit_length() - 1
    master_new, first_new, second, weight_new, copy = lax.switch(
        counter % bits,
        [partial(whole_step, bit) for bit in range(bits)],
        activations,
        cotangent,
        master[0],
        moment_one[0],
        moment_two[0],
        push_weight,
        scales,
    )
    return (master_new[None], first_new[None], second[None], weight_new, copy[None])


def solution(mesh):
    placed = (
        P(("rep", "fsdp"), None),
        P(("rep", "fsdp"), None),
        P("rep", "fsdp", None),
        P("rep", "fsdp", None),
        P("rep", "fsdp", None),
        P("rep"),
        P(),
    )
    return jax.shard_map(
        on_device,
        mesh=mesh,
        in_specs=placed,
        out_specs=(
            P("rep", "fsdp", None),
            P("rep", "fsdp", None),
            P("rep", "fsdp", None),
            P("rep"),
            P("rep", "fsdp", None),
        ),
        check_vma=False,
    )
```

```python
import math
from functools import partial

import jax
import jax.numpy as jnp
from jax import lax
from jax.experimental import pallas as pl
from jax.experimental.pallas import tpu as pltpu
from jax.sharding import PartitionSpec as P

BETA_ONE = 0.9
BETA_TWO = 0.95
LEARN_RATE = 0.01
DECAY_RATE = 0.1
EPSILON = 1e-08

F32 = jnp.float32
BF16 = jnp.bfloat16
HBM = pl.BlockSpec(memory_space=pltpu.HBM)
SMEM = pl.BlockSpec(memory_space=pltpu.SMEM)
VMEM = pl.BlockSpec(memory_space=pltpu.VMEM)
PARAMS = pltpu.CompilerParams(vmem_limit_bytes=16 * 1024 * 1024)
SMALL = pl.CostEstimate(flops=0, bytes_accessed=0, transcendentals=0)
CHUNKS = ((0, 256), (256, 256))
PARTS = 4


def shape(dtype, *sizes):
    return pltpu.VMEM(sizes, dtype)


def in_hbm(array):
    return pltpu.with_memory_space_constraint(array, pltpu.HBM)


def product(x, g):
    return lax.dot_general(x, g, (((0,), (0,)), ((), ())), preferred_element_type=F32)


class Blocks:
    def __init__(self, x, g, x_held, g_held, x_sems, g_sems, columns):
        tokens, width = x_held.shape[1:]
        part = tokens // PARTS
        rows = [pl.ds(i * part, part) for i in range(PARTS)]
        self.g_copies = [pltpu.make_async_copy(g.at[at], g_held.at[at], g_sems.at[i]) for i, at in enumerate(rows)]
        self.x_copies = [
            [
                pltpu.make_async_copy(
                    x.at[at, pl.ds(pl.multiple_of(low, width), width)], x_held.at[k, at], x_sems.at[PARTS * k + i]
                )
                for i, at in enumerate(rows)
            ]
            for k, low in enumerate(columns)
        ]
        self.x_held, self.g_held = x_held, g_held
        for copy in self.g_copies:
            copy.start()
        for copies in self.x_copies[:2]:
            for copy in copies:
                copy.start()

    def product(self, k):
        if k == 0:
            for copy in self.g_copies:
                copy.wait()
        for copy in self.x_copies[k]:
            copy.wait()
        for copies in self.x_copies[k + 2 : k + 3]:
            for copy in copies:
                copy.start()
        return product(self.x_held[k], self.g_held[...])

    @staticmethod
    def scratch(blocks, tokens, width, columns):
        return [
            pltpu.VMEM((blocks, tokens, width), BF16),
            pltpu.VMEM((tokens, columns), BF16),
            pltpu.SemaphoreType.DMA((PARTS * blocks,)),
            pltpu.SemaphoreType.DMA((PARTS,)),
        ]


def first_column(me, ahead, other, width, groups):
    group, core = lax.shift_right_logical(me[0], 1), lax.bitwise_and(me[0], 1)
    return (2 * lax.rem(group + ahead, groups) + (1 - core if other else core)) * width


def others_kernel(aheads, me, x, g, out, *scratch):
    width = out.shape[0] // len(aheads)
    groups = x.shape[1] // (2 * width)
    blocks = Blocks(x, g, *scratch, [first_column(me, d % groups, True, width, groups) for d in aheads])
    for k in range(len(aheads)):
        out[pl.ds(k * width, width)] = blocks.product(k).astype(BF16)


def other_blocks(aheads, me, x, g, width):
    tokens, columns = g.shape
    return pl.pallas_call(
        partial(others_kernel, aheads),
        in_specs=[SMEM, HBM, HBM],
        out_specs=VMEM,
        out_shape=shape(BF16, len(aheads) * width, columns),
        scratch_shapes=Blocks.scratch(len(aheads), tokens, width, columns),
        compiler_params=PARAMS,
        cost_estimate=SMALL,
        name="other_blocks",
    )(me, x, g)


def far_kernel(me, x, g, got, *rest):
    up, down, *scratch = rest
    width = got.shape[0]
    groups = x.shape[1] // (2 * width)
    total = Blocks(x, g, *scratch, [first_column(me, 2, False, width, groups)]).product(0) + got[...].astype(F32)
    to = 0
    for low, rows in CHUNKS:
        half = rows // 2
        up[to : to + half] = total[low : low + half].astype(BF16)
        down[to : to + half] = total[low + half : low + rows].astype(BF16)
        to += half


def far_block(me, x, g, got):
    outs = [shape(BF16, got.shape[0] // 2, g.shape[1])] * 2
    return pl.pallas_call(
        far_kernel,
        in_specs=[SMEM, HBM, HBM, VMEM],
        out_specs=[VMEM] * len(outs),
        out_shape=outs,
        scratch_shapes=Blocks.scratch(1, g.shape[0], *got.shape),
        compiler_params=PARAMS,
        cost_estimate=SMALL,
        name="far_block",
    )(me, x, g, got)


def near_kernel(me, x, g, got, *rest):
    b_up, b_down, c_up_1, c_down_1, c_up_2, c_down_2, own_1, own_2 = rest[:8]
    width = got.shape[0] // 3
    groups = x.shape[1] // (2 * width)
    blocks = Blocks(x, g, *rest[8:], [first_column(me, d, False, width, groups) for d in (1, groups - 1, 0)])
    (low_1, rows_1), (low_2, rows_2) = CHUNKS
    half_1, half_2 = rows_1 // 2, rows_2 // 2

    def total(k):
        return blocks.product(k) + got[pl.ds(k * width, width)].astype(F32)

    above = total(0)
    c_up_1[...] = above[low_1 : low_1 + half_1]
    b_up[:half_1] = above[low_1 + half_1 : low_1 + rows_1].astype(BF16)
    c_up_2[...] = above[low_2 : low_2 + half_2]
    b_up[half_1:] = above[low_2 + half_2 : low_2 + rows_2].astype(BF16)
    below = total(1)
    b_down[:half_1] = below[low_1 : low_1 + half_1].astype(BF16)
    c_down_1[...] = below[low_1 + half_1 : low_1 + rows_1]
    b_down[half_1:] = below[low_2 : low_2 + half_2].astype(BF16)
    c_down_2[...] = below[low_2 + half_2 : low_2 + rows_2]
    own = total(2)
    own_1[...] = own[low_1 : low_1 + rows_1]
    own_2[...] = own[low_2 : low_2 + rows_2]


def near_blocks(me, x, g, got):
    columns = g.shape[1]
    (_, rows_1), (_, rows_2) = CHUNKS
    half_1, half_2 = rows_1 // 2, rows_2 // 2
    outs = [shape(BF16, half_1 + half_2, columns)] * 2
    outs += [shape(F32, half_1, columns)] * 2 + [shape(F32, half_2, columns)] * 2
    outs += [shape(F32, rows_1, columns), jax.ShapeDtypeStruct((rows_2, columns), F32)]
    return pl.pallas_call(
        near_kernel,
        in_specs=[SMEM, HBM, HBM, VMEM],
        out_specs=[VMEM] * len(outs),
        out_shape=outs,
        scratch_shapes=Blocks.scratch(3, g.shape[0], got.shape[0] // 3, columns),
        compiler_params=PARAMS,
        cost_estimate=SMALL,
        name="near_blocks",
    )(me, x, g, got)


def add_kernel(low, up, got_up, down, got_down, *rest):
    at = pl.ds(low, up.shape[0])
    for mine, got, out in ((up, got_up, rest[-2]), (down, got_down, rest[-1])):
        out[...] = (mine[...] + got[at].astype(F32)).astype(BF16)


def add_far(low, up, got_up, down, got_down, earlier=()):
    return pl.pallas_call(
        partial(add_kernel, low),
        in_specs=[VMEM] * 4 + [HBM] * len(earlier),
        out_specs=[VMEM] * 2,
        out_shape=[shape(BF16, *up.shape)] * 2,
        compiler_params=PARAMS,
        cost_estimate=SMALL,
        name="add_far",
    )(up, got_up, down, got_down, *earlier)


def fetch_kernel(places, *refs):
    count = len(places)
    copies = []
    for i, (start, rows) in enumerate(places):
        source, held, sems = refs[i], refs[count + i], refs[2 * count]
        part = rows // 2
        for k in range(2):
            copies.append(
                pltpu.make_async_copy(
                    source.at[pl.ds(start + k * part, part)], held.at[pl.ds(k * part, part)], sems.at[2 * i + k]
                )
            )
            copies[-1].start()
    for copy in copies:
        copy.wait()


def fetch(places, *arrays):
    return pl.pallas_call(
        partial(fetch_kernel, places),
        in_specs=[HBM] * len(arrays),
        out_specs=[VMEM] * len(arrays),
        out_shape=[shape(a.dtype, rows, a.shape[1]) for a, (_, rows) in zip(arrays, places)],
        scratch_shapes=[pltpu.SemaphoreType.DMA((2 * len(arrays),))],
        compiler_params=PARAMS,
        cost_estimate=SMALL,
        name="fetch",
    )(*arrays)


def step_kernel(start, low_b, step, push_weight, own, c_up, c_down, b_up, b_down, master, one, two, *refs):
    second_out, halfway_out, first_out, send, second_made, halfway_made, first_made, sems = refs[-8:]
    copies = []
    rows, columns = own.shape
    half = rows // 2
    row = (1, columns)
    number = jnp.full(row, step[0] + 1, jnp.int32).astype(F32)
    scale_one = 1.0 / (1.0 - jnp.exp(number * math.log(BETA_ONE)))
    scale_two = 1.0 / (1.0 - jnp.exp(number * math.log(BETA_TWO)))
    decay = DECAY_RATE / jnp.full(row, push_weight[0], F32)
    for low, c, b in ((0, c_up, b_down), (half, c_down, b_up)):
        at = pl.ds(low, half)
        gradient = own[at] + (c[...].astype(F32) + b[pl.ds(low_b, half)].astype(F32))
        first = BETA_ONE * one[at] + (1.0 - BETA_ONE) * gradient
        second = BETA_TWO * two[at] + (1.0 - BETA_TWO) * gradient * gradient
        direction = first * scale_one / (jnp.sqrt(second * scale_two) + EPSILON)
        weights = master[at]
        halfway = weights - LEARN_RATE * (direction + weights * decay)
        second_made[at] = second
        halfway_made[at] = halfway
        first_made[at] = first
        send[at] = halfway.astype(BF16)
        send[pl.ds(rows + low, half)] = first.astype(BF16)
        for made, out, place in (
            (second_made, second_out, start + low),
            (halfway_made, halfway_out, low),
            (first_made, first_out, low),
        ):
            copies.append(pltpu.make_async_copy(made.at[at], out.at[pl.ds(place, half)], sems.at[len(copies)]))
            copies[-1].start()
    for copy in copies:
        copy.wait()


def step_chunk(start, height, low_b, ins, before=(), earlier=()):
    rows, columns = ins[2].shape
    return pl.pallas_call(
        partial(step_kernel, start, low_b),
        in_specs=[SMEM] * 2 + [VMEM] * (len(ins) - 2) + [HBM] * (len(before) + len(earlier)),
        out_specs=[HBM] * 3 + [VMEM],
        out_shape=[pltpu.HBM((height, columns), F32)]
        + [pltpu.HBM((rows, columns), F32)] * 2
        + [shape(BF16, 2 * rows, columns)],
        scratch_shapes=[pltpu.VMEM((rows, columns), F32)] * 3 + [pltpu.SemaphoreType.DMA((6,))],
        input_output_aliases={len(ins): 0} if before else {},
        compiler_params=PARAMS,
        cost_estimate=SMALL,
        name="step_chunk",
    )(*ins, *before, *earlier)


def mix_kernel(start, rows, push_weight, other_weight, halfway, first, got, *rest):
    master_out, first_out, copy_out, master_new, first_new, copy, in_sems, out_sems = rest[-8:]
    pieces = 2
    part = rows // pieces
    row = (1, got.shape[1])
    at = [pl.ds(k * part, part) for k in range(pieces)]
    to = [pl.ds(start + k * part, part) for k in range(pieces)]
    loads = [
        [
            pltpu.make_async_copy(source.at[at[k]], held.at[at[k]], in_sems.at[2 * k + i])
            for i, (source, held) in enumerate(((halfway, master_new), (first, first_new)))
        ]
        for k in range(pieces)
    ]
    for pair in loads:
        for load in pair:
            load.start()
    copies = []
    scale = 1.0 / (0.5 * (jnp.full(row, push_weight[0], F32) + jnp.full(row, other_weight[0], F32)))
    for k in range(pieces):
        for load in loads[k]:
            load.wait()
        mixed = 0.5 * (master_new[at[k]] + got[at[k]].astype(F32))
        master_new[at[k]] = mixed
        copy[at[k]] = (mixed * scale).astype(BF16)
        first_new[at[k]] = 0.5 * (first_new[at[k]] + got[pl.ds(rows + k * part, part)].astype(F32))
        for i, (made, out) in enumerate(((master_new, master_out), (first_new, first_out), (copy, copy_out))):
            send = pltpu.make_async_copy(made.at[at[k]], out.at[to[k]], out_sems.at[3 * k + i])
            send.start()
            copies.append(send)
    for send in copies:
        send.wait()


def mix_chunk(start, rows, height, push_weight, other_weight, halfway, first, got, before=()):
    columns = halfway.shape[1]
    ins = (push_weight, other_weight, in_hbm(halfway), in_hbm(first), got)
    return pl.pallas_call(
        partial(mix_kernel, start, rows),
        in_specs=[SMEM] * 2 + [HBM] * 2 + [VMEM] + [HBM] * len(before),
        out_specs=[HBM] * 3,
        out_shape=[pltpu.HBM((height, columns), F32)] * 2 + [pltpu.HBM((height, columns), BF16)],
        scratch_shapes=[
            pltpu.VMEM((rows, columns), F32),
            pltpu.VMEM((rows, columns), F32),
            pltpu.VMEM((rows, columns), BF16),
            pltpu.SemaphoreType.DMA((4,)),
            pltpu.SemaphoreType.DMA((6,)),
        ],
        input_output_aliases={len(ins) + i: i for i in range(len(before))},
        compiler_params=PARAMS,
        cost_estimate=SMALL,
        name="mix_chunk",
    )(*ins, *before)


def up_z(block):
    count = lax.axis_size("fsdp")
    return lax.ppermute(block, "fsdp", [(i, (i + 2) % count) for i in range(count)])


def down_z(block):
    count = lax.axis_size("fsdp")
    return lax.ppermute(block, "fsdp", [(i, (i - 2) % count) for i in range(count)])


def other_core(block):
    return lax.ppermute(block, "fsdp", [(i, i ^ 1) for i in range(lax.axis_size("fsdp"))])


def from_partner(block, bit):
    return lax.ppermute(block, "rep", [(i, i ^ (1 << bit)) for i in range(lax.axis_size("rep"))])


def after(value, *earlier):
    return lax.optimization_barrier((value, *earlier))[0]


def first_exchange(bit, send, push_weight):
    return from_partner(send, bit), from_partner(push_weight, bit)


def second_exchange(height, bit, send, *mix):
    return (from_partner(send, bit), *mix_chunk(*CHUNKS[0], height, *mix))


def on_device(activations, cotangent, master, moment_one, moment_two, push_weight, step_index):
    x, g, state = in_hbm(activations), in_hbm(cotangent), [in_hbm(v[0]) for v in (master, moment_one, moment_two)]
    height = master.shape[1]
    bits = lax.axis_size("rep").bit_length() - 1

    def with_partner(exchange, *values):
        return lax.switch(lax.rem(step_index[0], bits), [partial(exchange, bit) for bit in range(bits)], *values)

    me = jnp.full((1,), lax.axis_index("fsdp"), jnp.int32)
    (low_1, rows_1), (low_2, rows_2) = CHUNKS
    half_1, half_2 = rows_1 // 2, rows_2 // 2
    out_far = other_blocks((2,), me, x, g, height)
    out_near = other_blocks((1, -1, 0), after(me, out_far), x, g, height)
    got_far = other_core(out_far)
    got_near = other_core(after(out_near, got_far))
    a_up, a_down = far_block(after(me, out_near), x, g, got_far)
    got_a_up, got_a_down = up_z(a_up), down_z(a_down)
    state_1 = fetch([(low_1, rows_1)] * 3, *(after(v, a_up) for v in state))
    b_up, b_down, c_up_1, c_down_1, c_up_2, c_down_2, own_1, own_2 = near_blocks(
        me, x, g, after(got_near, state_1[0])
    )
    got_b = up_z(b_up), down_z(b_down)
    c_up_1, c_down_1 = add_far(0, c_up_1, got_a_up, c_down_1, got_a_down)
    got_c = up_z(c_up_1), down_z(c_down_1)
    rest = add_far(half_1, c_up_2, got_a_up, c_down_2, got_a_down, got_b)
    got_rest = up_z(rest[0]), down_z(rest[1])
    scalars = step_index, push_weight
    second, *made_1 = step_chunk(low_1, height, 0, (*scalars, own_1, *got_c, *got_b, *state_1), (), rest)
    got_1, other_weight = with_partner(first_exchange, made_1[2], push_weight)
    weights = push_weight, other_weight
    places_2 = [(low_2, rows_2)] * 3 + [(0, rows_2)]
    *state_2, own_2 = fetch(places_2, *(after(v, got_1) for v in (*state, own_2)))
    second, *made_2 = step_chunk(
        low_2, height, half_1, (*scalars, own_2, *got_rest, *got_b, *state_2), (second,)
    )
    got_2, *mixed = with_partner(partial(second_exchange, height), made_2[2], *weights, *made_1[:2], got_1)
    mixed, first, copy = mix_chunk(*CHUNKS[1], height, *weights, *made_2[:2], got_2, mixed)
    weight_new = 0.5 * (push_weight + other_weight)
    return (mixed[None], first[None], second[None], weight_new, copy[None])


def solution(mesh):
    placed = (
        P(("rep", "fsdp"), None),
        P(("rep", "fsdp"), None),
        P("rep", "fsdp", None),
        P("rep", "fsdp", None),
        P("rep", "fsdp", None),
        P("rep"),
        P(),
    )
    return jax.shard_map(
        on_device,
        mesh=mesh,
        in_specs=placed,
        out_specs=(
            P("rep", "fsdp", None),
            P("rep", "fsdp", None),
            P("rep", "fsdp", None),
            P("rep"),
            P("rep", "fsdp", None),
        ),
        check_vma=False,
    )
```

```python
import math
from functools import partial

import jax
import jax.numpy as jnp
from jax import lax
from jax.experimental import pallas as pl
from jax.experimental.pallas import tpu as pltpu
from jax.sharding import PartitionSpec as P

BETA_ONE = 0.9
BETA_TWO = 0.95
LEARN_RATE = 0.01
DECAY_RATE = 0.1
EPSILON = 1e-08

F32 = jnp.float32
BF16 = jnp.bfloat16
HBM = pl.BlockSpec(memory_space=pltpu.HBM)
SMEM = pl.BlockSpec(memory_space=pltpu.SMEM)
VMEM = pl.BlockSpec(memory_space=pltpu.VMEM)
PARAMS = pltpu.CompilerParams(vmem_limit_bytes=16 * 1024 * 1024)
SMALL = pl.CostEstimate(flops=0, bytes_accessed=0, transcendentals=0)
CHUNKS = ((0, 320), (320, 192))
PARTS = 4
TAIL = 16


def shape(dtype, *sizes):
    return pltpu.VMEM(sizes, dtype)


def in_hbm(array):
    return pltpu.with_memory_space_constraint(array, pltpu.HBM)


def product(x, g):
    return lax.dot_general(x, g, (((0,), (0,)), ((), ())), preferred_element_type=F32)


def first_column(me, ahead, other, width, groups):
    group, core = lax.shift_right_logical(me[0], 1), lax.bitwise_and(me[0], 1)
    low = (2 * lax.rem(group + ahead % groups, groups) + (1 - core if other else core)) * width
    return pl.multiple_of(low, width)


def row_copies(source, columns, held, sems, first):
    part = source.shape[0] // PARTS
    return [
        pltpu.make_async_copy(source.at[pl.ds(i * part, part), columns], held.at[pl.ds(i * part, part)], sems.at[first + i])
        for i in range(PARTS)
    ]


def start(copies):
    for copy in copies:
        copy.start()


def wait(copies):
    for copy in copies:
        copy.wait()


def first_kernel(me, x, g, out, g_held, x_held, sems):
    width, columns = out.shape
    groups = x.shape[1] // (2 * width)
    g_copies = row_copies(g, pl.ds(0, columns), g_held, sems, 0)
    x_copies = row_copies(x, pl.ds(first_column(me, 2, True, width, groups), width), x_held, sems, PARTS)
    start(g_copies)
    start(x_copies)
    wait(g_copies)
    wait(x_copies)
    out[...] = product(x_held[...], g_held[...]).astype(BF16)


def first_block(me, x, g, width):
    tokens, columns = g.shape
    return pl.pallas_call(
        first_kernel,
        in_specs=[SMEM, HBM, HBM],
        out_specs=[VMEM] * 2,
        out_shape=[shape(BF16, width, columns), shape(BF16, tokens, columns)],
        scratch_shapes=[pltpu.VMEM((tokens, width), BF16), pltpu.SemaphoreType.DMA((2 * PARTS,))],
        compiler_params=PARAMS,
        cost_estimate=SMALL,
        name="first_block",
    )(me, x, g)


def others_kernel(me, x, g, out, far, near, x_held, sems):
    width = far.shape[1]
    groups = x.shape[1] // (2 * width)

    def block(ahead, other, held, number):
        low = first_column(me, ahead, other, width, groups)
        return row_copies(x, pl.ds(low, width), held, sems, PARTS * number)

    aheads = (1, -1, 0)
    theirs = [block(ahead, True, x_held.at[k], k) for k, ahead in enumerate(aheads)]
    own = [block(2, False, far, 3)] + [block(ahead, False, near.at[k], 4 + k) for k, ahead in enumerate(aheads)]
    start(theirs[0])
    start(theirs[1])
    for k in range(3):
        wait(theirs[k])
        start(theirs[2] if k == 0 else own[0] if k == 1 else own[1])
        out[pl.ds(k * width, width)] = product(x_held[k], g[...]).astype(BF16)
    start(own[2])
    start(own[3])
    for copies in own:
        wait(copies)


def other_blocks(me, x, g, width):
    tokens, columns = g.shape
    return pl.pallas_call(
        others_kernel,
        in_specs=[SMEM, HBM, VMEM],
        out_specs=[VMEM] * 3,
        out_shape=[shape(BF16, 3 * width, columns), shape(BF16, tokens, width), shape(BF16, 3, tokens, width)],
        scratch_shapes=[pltpu.VMEM((3, tokens, width), BF16), pltpu.SemaphoreType.DMA((7 * PARTS,))],
        compiler_params=PARAMS,
        cost_estimate=SMALL,
        name="other_blocks",
    )(me, x, g)


def far_kernel(x, g, got, *outs):
    total = product(x[...], g[...]) + got[...].astype(F32)
    for k, (low, rows) in enumerate(CHUNKS):
        half = rows // 2
        outs[2 * k][...] = total[low : low + half].astype(BF16)
        outs[2 * k + 1][...] = total[low + half : low + rows].astype(BF16)


def far_block(x, g, got):
    columns = got.shape[1]
    return pl.pallas_call(
        far_kernel,
        in_specs=[VMEM] * 3,
        out_specs=[VMEM] * 4,
        out_shape=[shape(BF16, rows // 2, columns) for _, rows in CHUNKS for _ in range(2)],
        compiler_params=PARAMS,
        cost_estimate=SMALL,
        name="far_block",
    )(x, g, got)


def near_kernel(x, g, got, far_up, far_down, *outs):
    b_up, b_down, rest_up, rest_down, c_up_1, c_down_1, c_up_2, c_down_2, own_1, own_2 = outs
    width = got.shape[0] // 3
    (low_1, rows_1), (low_2, rows_2) = CHUNKS
    half_1, half_2 = rows_1 // 2, rows_2 // 2

    def total(k):
        return product(x[k], g[...]) + got[pl.ds(k * width, width)].astype(F32)

    def plain(values, chunk_1, chunk_2, far, b, rest):
        b[:half_2] = far[...]
        b[half_2:] = values[chunk_1 : chunk_1 + half_1].astype(BF16)
        rest[...] = values[chunk_2 : chunk_2 + half_2].astype(BF16)

    above = total(0)
    plain(above, low_1 + half_1, low_2 + half_2, far_up, b_up, rest_up)
    c_up_1[...] = above[low_1 : low_1 + half_1]
    c_up_2[...] = above[low_2 : low_2 + half_2]
    below = total(1)
    plain(below, low_1, low_2, far_down, b_down, rest_down)
    c_down_1[...] = below[low_1 + half_1 : low_1 + rows_1]
    c_down_2[...] = below[low_2 + half_2 : low_2 + rows_2]
    own = total(2)
    own_1[...] = own[low_1 : low_1 + rows_1]
    own_2[...] = own[low_2 : low_2 + rows_2]


def near_blocks(x, g, got, far_up, far_down):
    columns = g.shape[1]
    (_, rows_1), (_, rows_2) = CHUNKS
    half_1, half_2 = rows_1 // 2, rows_2 // 2
    outs = [shape(BF16, half_2 + half_1, columns)] * 2 + [shape(BF16, half_2, columns)] * 2
    outs += [shape(F32, half_1, columns)] * 2 + [shape(F32, half_2, columns)] * 2
    outs += [shape(F32, rows_1, columns), jax.ShapeDtypeStruct((rows_2, columns), F32)]
    return pl.pallas_call(
        near_kernel,
        in_specs=[VMEM] * 5,
        out_specs=[VMEM] * len(outs),
        out_shape=outs,
        compiler_params=PARAMS,
        cost_estimate=SMALL,
        name="near_blocks",
    )(x, g, got, far_up, far_down)


def add_kernel(low, count, up, got_up, down, got_down, *rest):
    more, outs = rest[:count], rest[-2:]
    half = up.shape[0]
    for mine, got, out in ((up, got_up, outs[0]), (down, got_down, outs[1])):
        out[:half] = (mine[...] + got[pl.ds(low, half)].astype(F32)).astype(BF16)
    for value, out in zip(more, outs):
        out[half:] = value[...]


def add_far(low, up, got_up, down, got_down, more=(), earlier=()):
    rows = up.shape[0] + (more[0].shape[0] if more else 0)
    return pl.pallas_call(
        partial(add_kernel, low, len(more)),
        in_specs=[VMEM] * (4 + len(more)) + [HBM] * len(earlier),
        out_specs=[VMEM] * 2,
        out_shape=[shape(BF16, rows, up.shape[1])] * 2,
        compiler_params=PARAMS,
        cost_estimate=SMALL,
        name="add_far",
    )(up, got_up, down, got_down, *more, *earlier)


def fetch_kernel(places, *refs):
    count = len(places)
    copies = []
    for i, (start, rows) in enumerate(places):
        source, held, sems = refs[i], refs[count + i], refs[2 * count]
        part = rows // 2
        for k in range(2):
            copies.append(
                pltpu.make_async_copy(
                    source.at[pl.ds(start + k * part, part)], held.at[pl.ds(k * part, part)], sems.at[2 * i + k]
                )
            )
            copies[-1].start()
    for copy in copies:
        copy.wait()


def fetch(places, *arrays):
    return pl.pallas_call(
        partial(fetch_kernel, places),
        in_specs=[HBM] * len(arrays),
        out_specs=[VMEM] * len(arrays),
        out_shape=[shape(a.dtype, rows, a.shape[1]) for a, (_, rows) in zip(arrays, places)],
        scratch_shapes=[pltpu.SemaphoreType.DMA((2 * len(arrays),))],
        compiler_params=PARAMS,
        cost_estimate=SMALL,
        name="fetch",
    )(*arrays)


def step_kernel(first_row, places, kept, step, push_weight, own, c_up, c_down, *refs):
    count = 1 + max(at for at, _, _ in places)
    b_ups, b_downs = refs[:count], refs[count : 2 * count]
    master, one, two = refs[2 * count : 2 * count + 3]
    if kept:
        second_out, halfway_made, first_made, send, second_made, sems = refs[-6:]
        away = [(second_made, second_out, first_row)]
    else:
        second_out, halfway_out, first_out, send, second_made, halfway_made, first_made, sems = refs[-8:]
        away = [(second_made, second_out, first_row), (halfway_made, halfway_out, 0), (first_made, first_out, 0)]
    copies = []
    rows, columns = own.shape
    line = lax.broadcasted_iota(jnp.int32, (TAIL, columns), 0)
    left = jnp.full((TAIL, columns), push_weight[0], F32)
    high = left.astype(BF16).astype(F32)
    middle = (left - high).astype(BF16).astype(F32)
    low = left - high - middle
    parts = jnp.where(line == 0, high, jnp.where(line == 1, middle, jnp.where(line == 2, low, 0.0)))
    send[pl.ds(2 * rows, TAIL)] = parts.astype(BF16)
    half = rows // 2
    row = (1, columns)
    number = jnp.full(row, step[0] + 1, jnp.int32).astype(F32)
    scale_one = 1.0 / (1.0 - jnp.exp(number * math.log(BETA_ONE)))
    scale_two = 1.0 / (1.0 - jnp.exp(number * math.log(BETA_TWO)))
    decay = DECAY_RATE / jnp.full(row, push_weight[0], F32)
    for low, c, b_pieces in ((0, c_up, b_downs), (half, c_down, b_ups)):
        to = 0
        for which, b_low, size in places:
            at = pl.ds(low + to, size)
            far = b_pieces[which][pl.ds(b_low, size)].astype(F32)
            gradient = own[at] + (c[pl.ds(to, size)].astype(F32) + far)
            first = BETA_ONE * one[at] + (1.0 - BETA_ONE) * gradient
            second = BETA_TWO * two[at] + (1.0 - BETA_TWO) * gradient * gradient
            direction = first * scale_one / (jnp.sqrt(second * scale_two) + EPSILON)
            weights = master[at]
            halfway = weights - LEARN_RATE * (direction + weights * decay)
            second_made[at] = second
            halfway_made[at] = halfway
            first_made[at] = first
            send[at] = halfway.astype(BF16)
            send[pl.ds(rows + low + to, size)] = first.astype(BF16)
            to += size
        at = pl.ds(low, half)
        for made, out, place in away:
            copies.append(pltpu.make_async_copy(made.at[at], out.at[pl.ds(place + low, half)], sems.at[len(copies)]))
            copies[-1].start()
    for copy in copies:
        copy.wait()


def step_chunk(first_row, height, places, kept, ins, before=(), earlier=()):
    rows, columns = ins[2].shape
    return pl.pallas_call(
        partial(step_kernel, first_row, places, kept),
        in_specs=[SMEM] * 2 + [VMEM] * (len(ins) - 2) + [HBM] * (len(before) + len(earlier)),
        out_specs=[HBM] + [VMEM if kept else HBM] * 2 + [VMEM],
        out_shape=[pltpu.HBM((height, columns), F32)]
        + [(pltpu.VMEM if kept else pltpu.HBM)((rows, columns), F32)] * 2
        + [shape(BF16, 2 * rows + TAIL, columns)],
        scratch_shapes=[pltpu.VMEM((rows, columns), F32)] * (1 if kept else 3) + [pltpu.SemaphoreType.DMA((6,))],
        input_output_aliases={len(ins): 0} if before else {},
        compiler_params=PARAMS,
        cost_estimate=SMALL,
        name="step_chunk",
    )(*ins, *before, *earlier)


def mixed_scale(push_weight, tail):
    return 1.0 / (0.5 * (push_weight[0] + jnp.sum(tail.astype(F32), axis=0, keepdims=True)))


def mix_kernel(first_row, rows, push_weight, halfway, first, got, *rest):
    master_out, first_out, copy_out, master_new, first_new, copy, in_sems, out_sems = rest[-8:]
    pieces = 4
    part = rows // pieces
    at = [pl.ds(k * part, part) for k in range(pieces)]
    behind = [pl.ds(rows + k * part, part) for k in range(pieces)]
    loads = [
        [
            pltpu.make_async_copy(source.at[at[k]], held.at[at[k]], in_sems.at[2 * k + i])
            for i, (source, held) in enumerate(((halfway, master_new), (first, first_new)))
        ]
        for k in range(pieces)
    ]
    for pair in loads:
        start(pair)
    sends = []
    scale = mixed_scale(push_weight, got[pl.ds(2 * rows, TAIL)])
    for k in range(pieces):
        wait(loads[k])
        mixed = 0.5 * (master_new[at[k]] + got[at[k]].astype(F32))
        master_new[at[k]] = mixed
        copy[at[k]] = (mixed * scale).astype(BF16)
        first_new[at[k]] = 0.5 * (first_new[at[k]] + got[behind[k]].astype(F32))
        to = pl.ds(first_row + k * part, part)
        sends.append(
            [
                pltpu.make_async_copy(made.at[at[k]], out.at[to], out_sems.at[3 * k + i])
                for i, (made, out) in enumerate(((master_new, master_out), (first_new, first_out), (copy, copy_out)))
            ]
        )
        start(sends[k])
    for three in sends:
        wait(three)


def mix_chunk(first_row, rows, height, push_weight, halfway, first, got, before=()):
    columns = halfway.shape[1]
    ins = (push_weight, in_hbm(halfway), in_hbm(first), got)
    return pl.pallas_call(
        partial(mix_kernel, first_row, rows),
        in_specs=[SMEM] + [HBM] * 2 + [VMEM] + [HBM] * len(before),
        out_specs=[HBM] * 3,
        out_shape=[pltpu.HBM((height, columns), F32)] * 2 + [pltpu.HBM((height, columns), BF16)],
        scratch_shapes=[
            pltpu.VMEM((rows, columns), F32),
            pltpu.VMEM((rows, columns), F32),
            pltpu.VMEM((rows, columns), BF16),
            pltpu.SemaphoreType.DMA((8,)),
            pltpu.SemaphoreType.DMA((12,)),
        ],
        input_output_aliases={len(ins) + i: i for i in range(len(before))},
        compiler_params=PARAMS,
        cost_estimate=SMALL,
        name="mix_chunk",
    )(*ins, *before)


def last_kernel(first_row, rows, push_weight, halfway, first, got, *rest):
    master_out, first_out, copy_out, master_new, first_new, copy, sems = rest[-7:]
    pieces = 2
    part = rows // pieces
    scale = mixed_scale(push_weight, got[pl.ds(2 * rows, TAIL)])
    sends = []
    for k in range(pieces):
        at, to = pl.ds(k * part, part), pl.ds(first_row + k * part, part)
        mixed = 0.5 * (halfway[at] + got[at].astype(F32))
        master_new[at] = mixed
        copy[at] = (mixed * scale).astype(BF16)
        first_new[at] = 0.5 * (first[at] + got[pl.ds(rows + k * part, part)].astype(F32))
        sends += [
            pltpu.make_async_copy(made.at[at], out.at[to], sems.at[3 * k + i])
            for i, (made, out) in enumerate(((master_new, master_out), (first_new, first_out), (copy, copy_out)))
        ]
        start(sends[3 * k :])
    wait(sends)


def last_mix(first_row, rows, height, push_weight, halfway, first, got, before):
    columns = halfway.shape[1]
    ins = (push_weight, halfway, first, got)
    return pl.pallas_call(
        partial(last_kernel, first_row, rows),
        in_specs=[SMEM] + [VMEM] * 3 + [HBM] * len(before),
        out_specs=[HBM] * 3,
        out_shape=[pltpu.HBM((height, columns), F32)] * 2 + [pltpu.HBM((height, columns), BF16)],
        scratch_shapes=[
            pltpu.VMEM((rows, columns), F32),
            pltpu.VMEM((rows, columns), F32),
            pltpu.VMEM((rows, columns), BF16),
            pltpu.SemaphoreType.DMA((6,)),
        ],
        input_output_aliases={len(ins) + i: i for i in range(len(before))},
        compiler_params=PARAMS,
        cost_estimate=SMALL,
        name="last_mix",
    )(*ins, *before)


def pass_kernel(*refs):
    refs[-1][0] = jnp.int32(0)


def passed(*arrays):
    return pl.pallas_call(
        pass_kernel,
        in_specs=[HBM] * len(arrays),
        out_specs=[HBM] * len(arrays),
        out_shape=[pltpu.HBM(a.shape, a.dtype) for a in arrays],
        scratch_shapes=[pltpu.SMEM((1,), jnp.int32)],
        input_output_aliases={i: i for i in range(len(arrays))},
        compiler_params=PARAMS,
        cost_estimate=SMALL,
        name="passed",
    )(*arrays)


def up_z(block):
    count = lax.axis_size("fsdp")
    return lax.ppermute(block, "fsdp", [(i, (i + 2) % count) for i in range(count)])


def down_z(block):
    count = lax.axis_size("fsdp")
    return lax.ppermute(block, "fsdp", [(i, (i - 2) % count) for i in range(count)])


def other_core(block):
    return lax.ppermute(block, "fsdp", [(i, i ^ 1) for i in range(lax.axis_size("fsdp"))])


def from_partner(block, bit):
    return lax.ppermute(block, "rep", [(i, i ^ (1 << bit)) for i in range(lax.axis_size("rep"))])


def after(value, *earlier):
    return lax.optimization_barrier((value, *earlier))[0]


def exchanges(height, bit, push_weight, step_index, send_1, halfway_1, first_1, second, rest_up, rest_down, own_2, *state):
    (low_2, rows_2), half_2 = CHUNKS[1], CHUNKS[1][1] // 2
    got_1 = from_partner(send_1, bit)
    got_rest = up_z(rest_up), down_z(rest_down)
    *state_2, own_2 = fetch(((low_2, rows_2),) * 3 + ((0, rows_2),), *(in_hbm(v) for v in (*state, own_2)))
    second, halfway_2, first_2, send_2 = step_chunk(
        low_2,
        height,
        ((0, half_2, half_2),),
        True,
        (step_index, push_weight, own_2, *got_rest, *got_rest, *state_2),
        (second,),
    )
    got_2 = from_partner(send_2, bit)
    other_weight = from_partner(push_weight, bit)
    mixed = mix_chunk(*CHUNKS[0], height, push_weight, halfway_1, first_1, got_1)
    return (other_weight, second, *last_mix(*CHUNKS[1], height, push_weight, halfway_2, first_2, got_2, mixed))


def on_device(activations, cotangent, master, moment_one, moment_two, push_weight, step_index):
    x, g, state = in_hbm(activations), in_hbm(cotangent), [in_hbm(v[0]) for v in (master, moment_one, moment_two)]
    height = master.shape[1]
    bits = lax.axis_size("rep").bit_length() - 1

    me = jnp.full((1,), lax.axis_index("fsdp"), jnp.int32)
    (low_1, rows_1), (low_2, rows_2) = CHUNKS
    half_1, half_2 = rows_1 // 2, rows_2 // 2
    out_far, g_held = first_block(me, x, g, height)
    got_far = other_core(out_far)
    out_near, x_far, x_near = other_blocks(me, x, g_held, height)
    got_near = other_core(after(out_near, got_far))
    a_up_1, a_down_1, a_up_2, a_down_2 = far_block(x_far, g_held, got_far)
    got_a_up, got_a_down = up_z(a_up_1), down_z(a_down_1)
    b_up, b_down, *later, c_up_1, c_down_1, c_up_2, c_down_2, own_1, own_2 = near_blocks(
        x_near, g_held, got_near, a_up_2, a_down_2
    )
    got_b = up_z(b_up), down_z(b_down)
    state_1 = fetch([(low_1, rows_1)] * 3, *(after(v, b_up) for v in state))
    c_up_1, c_down_1 = add_far(0, c_up_1, got_a_up, c_down_1, got_a_down)
    got_c = up_z(c_up_1), down_z(c_down_1)
    rest = add_far(0, c_up_2, got_b[0], c_down_2, got_b[1], later, (*got_c, state_1[0]))
    second, *made_1 = step_chunk(
        low_1, height, ((0, half_2, half_1),), False, (step_index, push_weight, own_1, *got_c, *got_b, *state_1)
    )
    other_weight, *made = lax.switch(
        lax.rem(step_index[0], bits),
        [partial(exchanges, height, bit) for bit in range(bits)],
        push_weight,
        step_index,
        made_1[2],
        *made_1[:2],
        second,
        *rest,
        own_2,
        *state,
    )
    second, mixed, first, copy = passed(*made)
    weight_new = 0.5 * (push_weight + other_weight)
    return (mixed[None], first[None], second[None], weight_new, copy[None])


def solution(mesh):
    placed = (
        P(("rep", "fsdp"), None),
        P(("rep", "fsdp"), None),
        P("rep", "fsdp", None),
        P("rep", "fsdp", None),
        P("rep", "fsdp", None),
        P("rep"),
        P(),
    )
    return jax.shard_map(
        on_device,
        mesh=mesh,
        in_specs=placed,
        out_specs=(
            P("rep", "fsdp", None),
            P("rep", "fsdp", None),
            P("rep", "fsdp", None),
            P("rep"),
            P("rep", "fsdp", None),
        ),
        check_vma=False,
    )
```

```python
import math
from functools import partial

import jax
import jax.numpy as jnp
from jax import lax
from jax.experimental import pallas as pl
from jax.experimental.pallas import tpu as pltpu
from jax.sharding import PartitionSpec as P

BETA_ONE = 0.9
BETA_TWO = 0.95
LEARN_RATE = 0.01
DECAY_RATE = 0.1
EPSILON = 1e-08

F32 = jnp.float32
BF16 = jnp.bfloat16
HBM = pl.BlockSpec(memory_space=pltpu.HBM)
SMEM = pl.BlockSpec(memory_space=pltpu.SMEM)
VMEM = pl.BlockSpec(memory_space=pltpu.VMEM)
PARAMS = pltpu.CompilerParams(vmem_limit_bytes=16 * 1024 * 1024)
SMALL = pl.CostEstimate(flops=0, bytes_accessed=0, transcendentals=0)
CHUNKS = ((0, 320), (320, 192))
PARTS = 4
TAIL = 16


def shape(dtype, *sizes):
    return pltpu.VMEM(sizes, dtype)


def in_hbm(array):
    return pltpu.with_memory_space_constraint(array, pltpu.HBM)


def product(x, g):
    return lax.dot_general(x, g, (((0,), (0,)), ((), ())), preferred_element_type=F32)


def first_column(me, ahead, other, width, groups):
    group, core = lax.shift_right_logical(me[0], 1), lax.bitwise_and(me[0], 1)
    low = (2 * lax.rem(group + ahead % groups, groups) + (1 - core if other else core)) * width
    return pl.multiple_of(low, width)


def row_copies(source, columns, held, sems, first):
    part = source.shape[0] // PARTS
    return [
        pltpu.make_async_copy(source.at[pl.ds(i * part, part), columns], held.at[pl.ds(i * part, part)], sems.at[first + i])
        for i in range(PARTS)
    ]


def start(copies):
    for copy in copies:
        copy.start()


def wait(copies):
    for copy in copies:
        copy.wait()


def first_kernel(me, x, g, out, g_held, x_held, sems):
    width, columns = out.shape
    groups = x.shape[1] // (2 * width)
    g_copies = row_copies(g, pl.ds(0, columns), g_held, sems, 0)
    x_copies = row_copies(x, pl.ds(first_column(me, 2, True, width, groups), width), x_held, sems, PARTS)
    start(g_copies)
    start(x_copies)
    wait(g_copies)
    wait(x_copies)
    out[...] = product(x_held[...], g_held[...]).astype(BF16)


def first_block(me, x, g, width):
    tokens, columns = g.shape
    return pl.pallas_call(
        first_kernel,
        in_specs=[SMEM, HBM, HBM],
        out_specs=[VMEM] * 2,
        out_shape=[shape(BF16, width, columns), shape(BF16, tokens, columns)],
        scratch_shapes=[pltpu.VMEM((tokens, width), BF16), pltpu.SemaphoreType.DMA((2 * PARTS,))],
        compiler_params=PARAMS,
        cost_estimate=SMALL,
        name="first_block",
    )(me, x, g)


def others_kernel(me, x, g, out, far, near, x_held, sems):
    width = far.shape[1]
    groups = x.shape[1] // (2 * width)

    def block(ahead, other, held, number):
        low = first_column(me, ahead, other, width, groups)
        return row_copies(x, pl.ds(low, width), held, sems, PARTS * number)

    aheads = (1, -1, 0)
    theirs = [block(ahead, True, x_held.at[k], k) for k, ahead in enumerate(aheads)]
    own = [block(2, False, far, 3)] + [block(ahead, False, near.at[k], 4 + k) for k, ahead in enumerate(aheads)]
    start(theirs[0])
    start(theirs[1])
    for k in range(3):
        wait(theirs[k])
        start(theirs[2] if k == 0 else own[0] if k == 1 else own[1])
        out[pl.ds(k * width, width)] = product(x_held[k], g[...]).astype(BF16)
    start(own[2])
    start(own[3])
    for copies in own:
        wait(copies)


def other_blocks(me, x, g, width):
    tokens, columns = g.shape
    return pl.pallas_call(
        others_kernel,
        in_specs=[SMEM, HBM, VMEM],
        out_specs=[VMEM] * 3,
        out_shape=[shape(BF16, 3 * width, columns), shape(BF16, tokens, width), shape(BF16, 3, tokens, width)],
        scratch_shapes=[pltpu.VMEM((3, tokens, width), BF16), pltpu.SemaphoreType.DMA((7 * PARTS,))],
        compiler_params=PARAMS,
        cost_estimate=SMALL,
        name="other_blocks",
    )(me, x, g)


def far_kernel(x, g, got, *outs):
    total = product(x[...], g[...]) + got[...].astype(F32)
    for k, (low, rows) in enumerate(CHUNKS):
        half = rows // 2
        outs[2 * k][...] = total[low : low + half].astype(BF16)
        outs[2 * k + 1][...] = total[low + half : low + rows].astype(BF16)


def far_block(x, g, got):
    columns = got.shape[1]
    return pl.pallas_call(
        far_kernel,
        in_specs=[VMEM] * 3,
        out_specs=[VMEM] * 4,
        out_shape=[shape(BF16, rows // 2, columns) for _, rows in CHUNKS for _ in range(2)],
        compiler_params=PARAMS,
        cost_estimate=SMALL,
        name="far_block",
    )(x, g, got)


def near_kernel(x, g, got, far_up, far_down, *outs):
    b_up, b_down, rest_up, rest_down, c_up_1, c_down_1, c_up_2, c_down_2, own_1, own_2 = outs
    width = got.shape[0] // 3
    (low_1, rows_1), (low_2, rows_2) = CHUNKS
    half_1, half_2 = rows_1 // 2, rows_2 // 2

    def total(k):
        return product(x[k], g[...]) + got[pl.ds(k * width, width)].astype(F32)

    def plain(values, chunk_1, chunk_2, far, b, rest):
        b[:half_2] = far[...]
        b[half_2:] = values[chunk_1 : chunk_1 + half_1].astype(BF16)
        rest[...] = values[chunk_2 : chunk_2 + half_2].astype(BF16)

    above = total(0)
    plain(above, low_1 + half_1, low_2 + half_2, far_up, b_up, rest_up)
    c_up_1[...] = above[low_1 : low_1 + half_1]
    c_up_2[...] = above[low_2 : low_2 + half_2]
    below = total(1)
    plain(below, low_1, low_2, far_down, b_down, rest_down)
    c_down_1[...] = below[low_1 + half_1 : low_1 + rows_1]
    c_down_2[...] = below[low_2 + half_2 : low_2 + rows_2]
    own = total(2)
    own_1[...] = own[low_1 : low_1 + rows_1]
    own_2[...] = own[low_2 : low_2 + rows_2]


def near_blocks(x, g, got, far_up, far_down):
    columns = g.shape[1]
    (_, rows_1), (_, rows_2) = CHUNKS
    half_1, half_2 = rows_1 // 2, rows_2 // 2
    outs = [shape(BF16, half_2 + half_1, columns)] * 2 + [shape(BF16, half_2, columns)] * 2
    outs += [shape(F32, half_1, columns)] * 2 + [shape(F32, half_2, columns)] * 2
    outs += [shape(F32, rows_1, columns), jax.ShapeDtypeStruct((rows_2, columns), F32)]
    return pl.pallas_call(
        near_kernel,
        in_specs=[VMEM] * 5,
        out_specs=[VMEM] * len(outs),
        out_shape=outs,
        compiler_params=PARAMS,
        cost_estimate=SMALL,
        name="near_blocks",
    )(x, g, got, far_up, far_down)


def add_kernel(low, count, up, got_up, down, got_down, *rest):
    more, outs = rest[:count], rest[-2:]
    half = up.shape[0]
    for mine, got, out in ((up, got_up, outs[0]), (down, got_down, outs[1])):
        out[:half] = (mine[...] + got[pl.ds(low, half)].astype(F32)).astype(BF16)
    for value, out in zip(more, outs):
        out[half:] = value[...]


def add_far(low, up, got_up, down, got_down, more=(), earlier=()):
    rows = up.shape[0] + (more[0].shape[0] if more else 0)
    return pl.pallas_call(
        partial(add_kernel, low, len(more)),
        in_specs=[VMEM] * (4 + len(more)) + [HBM] * len(earlier),
        out_specs=[VMEM] * 2,
        out_shape=[shape(BF16, rows, up.shape[1])] * 2,
        compiler_params=PARAMS,
        cost_estimate=SMALL,
        name="add_far",
    )(up, got_up, down, got_down, *more, *earlier)


def fetch_kernel(places, *refs):
    count = len(places)
    copies = []
    for i, (start, rows) in enumerate(places):
        source, held, sems = refs[i], refs[count + i], refs[2 * count]
        part = rows // 2
        for k in range(2):
            copies.append(
                pltpu.make_async_copy(
                    source.at[pl.ds(start + k * part, part)], held.at[pl.ds(k * part, part)], sems.at[2 * i + k]
                )
            )
            copies[-1].start()
    for copy in copies:
        copy.wait()


def fetch(places, *arrays):
    return pl.pallas_call(
        partial(fetch_kernel, places),
        in_specs=[HBM] * len(arrays),
        out_specs=[VMEM] * len(arrays),
        out_shape=[shape(a.dtype, rows, a.shape[1]) for a, (_, rows) in zip(arrays, places)],
        scratch_shapes=[pltpu.SemaphoreType.DMA((2 * len(arrays),))],
        compiler_params=PARAMS,
        cost_estimate=SMALL,
        name="fetch",
    )(*arrays)


def step_kernel(first_row, places, step, push_weight, own, c_up, c_down, *refs):
    count = max(at for at, _, _ in places)
    b_ups, b_downs = (c_up, *refs[:count]), (c_down, *refs[count : 2 * count])
    master, one, two = refs[2 * count : 2 * count + 3]
    second_out, halfway_out, first_out, send, second_made, sems = refs[-6:]
    copies = []
    rows, columns = own.shape
    line = lax.broadcasted_iota(jnp.int32, (TAIL, columns), 0)
    left = jnp.full((TAIL, columns), push_weight[0], F32)
    high = left.astype(BF16).astype(F32)
    middle = (left - high).astype(BF16).astype(F32)
    low = left - high - middle
    parts = jnp.where(line == 0, high, jnp.where(line == 1, middle, jnp.where(line == 2, low, 0.0)))
    send[pl.ds(2 * rows, TAIL)] = parts.astype(BF16)
    half = rows // 2
    row = (1, columns)
    number = jnp.full(row, step[0] + 1, jnp.int32).astype(F32)
    scale_one = 1.0 / (1.0 - jnp.exp(number * math.log(BETA_ONE)))
    scale_two = 1.0 / (1.0 - jnp.exp(number * math.log(BETA_TWO)))
    decay = DECAY_RATE / jnp.full(row, push_weight[0], F32)
    for low, c, b_pieces in ((0, c_up, b_downs), (half, c_down, b_ups)):
        to = 0
        for which, b_low, size in places:
            at = pl.ds(low + to, size)
            far = b_pieces[which][pl.ds(b_low, size)].astype(F32)
            gradient = own[at] + (c[pl.ds(to, size)].astype(F32) + far)
            first = BETA_ONE * one[at] + (1.0 - BETA_ONE) * gradient
            second = BETA_TWO * two[at] + (1.0 - BETA_TWO) * gradient * gradient
            direction = first * scale_one / (jnp.sqrt(second * scale_two) + EPSILON)
            weights = master[at]
            halfway = weights - LEARN_RATE * (direction + weights * decay)
            second_made[at] = second
            halfway_out[at] = halfway
            first_out[at] = first
            send[at] = halfway.astype(BF16)
            send[pl.ds(rows + low + to, size)] = first.astype(BF16)
            to += size
        at = pl.ds(low, half)
        copies.append(
            pltpu.make_async_copy(second_made.at[at], second_out.at[pl.ds(first_row + low, half)], sems.at[len(copies)])
        )
        copies[-1].start()
    for copy in copies:
        copy.wait()


def step_chunk(first_row, height, places, ins, before=(), earlier=()):
    rows, columns = ins[2].shape
    return pl.pallas_call(
        partial(step_kernel, first_row, places),
        in_specs=[SMEM] * 2 + [VMEM] * (len(ins) - 2) + [HBM] * (len(before) + len(earlier)),
        out_specs=[HBM] + [VMEM] * 3,
        out_shape=[pltpu.HBM((height, columns), F32)]
        + [shape(F32, rows, columns)] * 2
        + [shape(BF16, 2 * rows + TAIL, columns)],
        scratch_shapes=[pltpu.VMEM((rows, columns), F32), pltpu.SemaphoreType.DMA((2,))],
        input_output_aliases={len(ins): 0} if before else {},
        compiler_params=PARAMS,
        cost_estimate=SMALL,
        name="step_chunk",
    )(*ins, *before, *earlier)


def mixed_scale(push_weight, tail):
    return 1.0 / (0.5 * (push_weight[0] + jnp.sum(tail.astype(F32), axis=0, keepdims=True)))


def mix_kernel(first_row, rows, push_weight, halfway, first, got, *rest):
    master_out, first_out, copy_out, master_new, first_new, copy, sems = rest[-7:]
    pieces = 2
    part = rows // pieces
    scale = mixed_scale(push_weight, got[pl.ds(2 * rows, TAIL)])
    sends = []
    for k in range(pieces):
        at, to = pl.ds(k * part, part), pl.ds(first_row + k * part, part)
        mixed = 0.5 * (halfway[at] + got[at].astype(F32))
        master_new[at] = mixed
        copy[at] = (mixed * scale).astype(BF16)
        first_new[at] = 0.5 * (first[at] + got[pl.ds(rows + k * part, part)].astype(F32))
        sends += [
            pltpu.make_async_copy(made.at[at], out.at[to], sems.at[3 * k + i])
            for i, (made, out) in enumerate(((master_new, master_out), (first_new, first_out), (copy, copy_out)))
        ]
        start(sends[3 * k :])
    wait(sends)


def mix_chunk(first_row, rows, height, push_weight, halfway, first, got, before=()):
    columns = halfway.shape[1]
    ins = (push_weight, halfway, first, got)
    return pl.pallas_call(
        partial(mix_kernel, first_row, rows),
        in_specs=[SMEM] + [VMEM] * 3 + [HBM] * len(before),
        out_specs=[HBM] * 3,
        out_shape=[pltpu.HBM((height, columns), F32)] * 2 + [pltpu.HBM((height, columns), BF16)],
        scratch_shapes=[
            pltpu.VMEM((rows, columns), F32),
            pltpu.VMEM((rows, columns), F32),
            pltpu.VMEM((rows, columns), BF16),
            pltpu.SemaphoreType.DMA((6,)),
        ],
        input_output_aliases={len(ins) + i: i for i in range(len(before))},
        compiler_params=PARAMS,
        cost_estimate=SMALL,
        name="mix_chunk",
    )(*ins, *before)


def pass_kernel(*refs):
    refs[-1][0] = jnp.int32(0)


def passed(*arrays):
    return pl.pallas_call(
        pass_kernel,
        in_specs=[HBM] * len(arrays),
        out_specs=[HBM] * len(arrays),
        out_shape=[pltpu.HBM(a.shape, a.dtype) for a in arrays],
        scratch_shapes=[pltpu.SMEM((1,), jnp.int32)],
        input_output_aliases={i: i for i in range(len(arrays))},
        compiler_params=PARAMS,
        cost_estimate=SMALL,
        name="passed",
    )(*arrays)


def up_z(block):
    count = lax.axis_size("fsdp")
    return lax.ppermute(block, "fsdp", [(i, (i + 2) % count) for i in range(count)])


def down_z(block):
    count = lax.axis_size("fsdp")
    return lax.ppermute(block, "fsdp", [(i, (i - 2) % count) for i in range(count)])


def other_core(block):
    return lax.ppermute(block, "fsdp", [(i, i ^ 1) for i in range(lax.axis_size("fsdp"))])


def from_partner(block, bit):
    return lax.ppermute(block, "rep", [(i, i ^ (1 << bit)) for i in range(lax.axis_size("rep"))])


def after(value, *earlier):
    return lax.optimization_barrier((value, *earlier))[0]


def exchanges(height, bit, push_weight, step_index, send_1, halfway_1, first_1, second, rest_up, rest_down, own_2, *state):
    (low_2, rows_2), half_2 = CHUNKS[1], CHUNKS[1][1] // 2
    got_1 = from_partner(send_1, bit)
    got_rest = up_z(rest_up), down_z(rest_down)
    *state_2, own_2 = fetch(((low_2, rows_2),) * 3 + ((0, rows_2),), *(in_hbm(v) for v in (*state, own_2)))
    second, halfway_2, first_2, send_2 = step_chunk(
        low_2,
        height,
        ((0, half_2, half_2),),
        (step_index, push_weight, own_2, *got_rest, *state_2),
        (second,),
    )
    got_2 = from_partner(send_2, bit)
    other_weight = from_partner(push_weight, bit)
    mixed = mix_chunk(*CHUNKS[0], height, push_weight, halfway_1, first_1, got_1)
    return (other_weight, second, *mix_chunk(*CHUNKS[1], height, push_weight, halfway_2, first_2, got_2, mixed))


def on_device(activations, cotangent, master, moment_one, moment_two, push_weight, step_index):
    x, g, state = in_hbm(activations), in_hbm(cotangent), [in_hbm(v[0]) for v in (master, moment_one, moment_two)]
    height = master.shape[1]
    bits = lax.axis_size("rep").bit_length() - 1

    me = jnp.full((1,), lax.axis_index("fsdp"), jnp.int32)
    (low_1, rows_1), (low_2, rows_2) = CHUNKS
    half_1, half_2 = rows_1 // 2, rows_2 // 2
    out_far, g_held = first_block(me, x, g, height)
    got_far = other_core(out_far)
    out_near, x_far, x_near = other_blocks(me, x, g_held, height)
    got_near = other_core(after(out_near, got_far))
    a_up_1, a_down_1, a_up_2, a_down_2 = far_block(x_far, g_held, got_far)
    got_a_up, got_a_down = up_z(a_up_1), down_z(a_down_1)
    b_up, b_down, *later, c_up_1, c_down_1, c_up_2, c_down_2, own_1, own_2 = near_blocks(
        x_near, g_held, got_near, a_up_2, a_down_2
    )
    got_b = up_z(b_up), down_z(b_down)
    state_1 = fetch([(low_1, rows_1)] * 3, *(after(v, b_up) for v in state))
    c_up_1, c_down_1 = add_far(0, c_up_1, got_a_up, c_down_1, got_a_down)
    got_c = up_z(c_up_1), down_z(c_down_1)
    rest = add_far(0, c_up_2, got_b[0], c_down_2, got_b[1], later, (*got_c, state_1[0]))
    second, *made_1 = step_chunk(
        low_1, height, ((1, half_2, half_1),), (step_index, push_weight, own_1, *got_c, *got_b, *state_1)
    )
    other_weight, *made = lax.switch(
        lax.rem(step_index[0], bits),
        [partial(exchanges, height, bit) for bit in range(bits)],
        push_weight,
        step_index,
        made_1[2],
        *made_1[:2],
        second,
        *rest,
        own_2,
        *state,
    )
    second, mixed, first, copy = passed(*made)
    weight_new = 0.5 * (push_weight + other_weight)
    return (mixed[None], first[None], second[None], weight_new, copy[None])


def solution(mesh):
    placed = (
        P(("rep", "fsdp"), None),
        P(("rep", "fsdp"), None),
        P("rep", "fsdp", None),
        P("rep", "fsdp", None),
        P("rep", "fsdp", None),
        P("rep"),
        P(),
    )
    return jax.shard_map(
        on_device,
        mesh=mesh,
        in_specs=placed,
        out_specs=(
            P("rep", "fsdp", None),
            P("rep", "fsdp", None),
            P("rep", "fsdp", None),
            P("rep"),
            P("rep", "fsdp", None),
        ),
        check_vma=False,
    )
```

```python
import math
from functools import partial

import jax
import jax.numpy as jnp
from jax import lax
from jax.experimental import pallas as pl
from jax.experimental.pallas import tpu as pltpu
from jax.sharding import PartitionSpec as P

BETA_ONE = 0.9
BETA_TWO = 0.95
LEARN_RATE = 0.01
DECAY_RATE = 0.1
EPSILON = 1e-08

F32 = jnp.float32
BF16 = jnp.bfloat16
HBM = pl.BlockSpec(memory_space=pltpu.HBM)
SMEM = pl.BlockSpec(memory_space=pltpu.SMEM)
VMEM = pl.BlockSpec(memory_space=pltpu.VMEM)
PARAMS = pltpu.CompilerParams(vmem_limit_bytes=16 * 1024 * 1024)
SMALL = pl.CostEstimate(flops=0, bytes_accessed=0, transcendentals=0)
CHUNKS = ((0, 320), (320, 192))
PARTS = 4
TAIL = 16


def shape(dtype, *sizes):
    return pltpu.VMEM(sizes, dtype)


def in_hbm(array):
    return pltpu.with_memory_space_constraint(array, pltpu.HBM)


def product(x, g):
    return lax.dot_general(x, g, (((0,), (0,)), ((), ())), preferred_element_type=F32)


def first_column(me, ahead, other, width, groups):
    group, core = lax.shift_right_logical(me[0], 1), lax.bitwise_and(me[0], 1)
    low = (2 * lax.rem(group + ahead % groups, groups) + (1 - core if other else core)) * width
    return pl.multiple_of(low, width)


def row_copies(source, columns, held, sems, first):
    part = source.shape[0] // PARTS
    return [
        pltpu.make_async_copy(source.at[pl.ds(i * part, part), columns], held.at[pl.ds(i * part, part)], sems.at[first + i])
        for i in range(PARTS)
    ]


def start(copies):
    for copy in copies:
        copy.start()


def wait(copies):
    for copy in copies:
        copy.wait()


def first_kernel(me, x, g, out, g_held, x_held, sems):
    width, columns = out.shape
    groups = x.shape[1] // (2 * width)
    g_copies = row_copies(g, pl.ds(0, columns), g_held, sems, 0)
    x_copies = row_copies(x, pl.ds(first_column(me, 2, True, width, groups), width), x_held, sems, PARTS)
    start(g_copies)
    start(x_copies)
    wait(g_copies)
    wait(x_copies)
    out[...] = product(x_held[...], g_held[...]).astype(BF16)


def first_block(me, x, g, width):
    tokens, columns = g.shape
    return pl.pallas_call(
        first_kernel,
        in_specs=[SMEM, HBM, HBM],
        out_specs=[VMEM] * 2,
        out_shape=[shape(BF16, width, columns), shape(BF16, tokens, columns)],
        scratch_shapes=[pltpu.VMEM((tokens, width), BF16), pltpu.SemaphoreType.DMA((2 * PARTS,))],
        compiler_params=PARAMS,
        cost_estimate=SMALL,
        name="first_block",
    )(me, x, g)


def column_blocks(me, x, other, held, sems, width):
    groups = x.shape[1] // (2 * width)
    return [
        row_copies(x, pl.ds(first_column(me, ahead, other, width, groups), width), held.at[k], sems, PARTS * k)
        for k, ahead in enumerate((1, -1, 0))
    ]


def others_kernel(me, x, g, out, far, x_held, sems):
    width = far.shape[1]
    groups = x.shape[1] // (2 * width)
    theirs = column_blocks(me, x, True, x_held, sems, width)
    own = row_copies(x, pl.ds(first_column(me, 2, False, width, groups), width), far, sems, 3 * PARTS)
    start(theirs[0])
    start(theirs[1])
    for k in range(3):
        wait(theirs[k])
        if k < 2:
            start((theirs[2], own)[k])
        out[pl.ds(k * width, width)] = product(x_held[k], g[...]).astype(BF16)
    wait(own)


def other_blocks(me, x, g, width):
    tokens, columns = g.shape
    return pl.pallas_call(
        others_kernel,
        in_specs=[SMEM, HBM, VMEM],
        out_specs=[VMEM] * 2,
        out_shape=[shape(BF16, 3 * width, columns), shape(BF16, tokens, width)],
        scratch_shapes=[pltpu.VMEM((3, tokens, width), BF16), pltpu.SemaphoreType.DMA((4 * PARTS,))],
        compiler_params=PARAMS,
        cost_estimate=SMALL,
        name="other_blocks",
    )(me, x, g)


def far_kernel(x, g, got, *outs):
    total = product(x[...], g[...]) + got[...].astype(F32)
    for k, (low, rows) in enumerate(CHUNKS):
        half = rows // 2
        outs[2 * k][...] = total[low : low + half].astype(BF16)
        outs[2 * k + 1][...] = total[low + half : low + rows].astype(BF16)


def far_block(x, g, got):
    columns = got.shape[1]
    return pl.pallas_call(
        far_kernel,
        in_specs=[VMEM] * 3,
        out_specs=[VMEM] * 4,
        out_shape=[shape(BF16, rows // 2, columns) for _, rows in CHUNKS for _ in range(2)],
        compiler_params=PARAMS,
        cost_estimate=SMALL,
        name="far_block",
    )(x, g, got)


def near_kernel(me, x, g, got, far_up, far_down, *outs):
    *outs, x_held, sems = outs
    b_up, b_down, rest_up, rest_down, c_up_1, c_down_1, c_up_2, c_down_2, own_1, own_2 = outs
    width = got.shape[0] // 3
    (low_1, rows_1), (low_2, rows_2) = CHUNKS
    half_1, half_2 = rows_1 // 2, rows_2 // 2

    blocks = column_blocks(me, x, False, x_held, sems, width)
    for copies in blocks:
        start(copies)

    def total(k):
        wait(blocks[k])
        return product(x_held[k], g[...]) + got[pl.ds(k * width, width)].astype(F32)

    def plain(values, chunk_1, chunk_2, far, b, rest):
        b[:half_2] = far[...]
        b[half_2:] = values[chunk_1 : chunk_1 + half_1].astype(BF16)
        rest[...] = values[chunk_2 : chunk_2 + half_2].astype(BF16)

    above = total(0)
    plain(above, low_1 + half_1, low_2 + half_2, far_up, b_up, rest_up)
    c_up_1[...] = above[low_1 : low_1 + half_1]
    c_up_2[...] = above[low_2 : low_2 + half_2]
    below = total(1)
    plain(below, low_1, low_2, far_down, b_down, rest_down)
    c_down_1[...] = below[low_1 + half_1 : low_1 + rows_1]
    c_down_2[...] = below[low_2 + half_2 : low_2 + rows_2]
    own = total(2)
    own_1[...] = own[low_1 : low_1 + rows_1]
    own_2[...] = own[low_2 : low_2 + rows_2]


def near_blocks(me, x, g, got, far_up, far_down):
    columns = g.shape[1]
    (_, rows_1), (_, rows_2) = CHUNKS
    half_1, half_2 = rows_1 // 2, rows_2 // 2
    outs = [shape(BF16, half_2 + half_1, columns)] * 2 + [shape(BF16, half_2, columns)] * 2
    outs += [shape(F32, half_1, columns)] * 2 + [shape(F32, half_2, columns)] * 2
    outs += [shape(F32, rows_1, columns), jax.ShapeDtypeStruct((rows_2, columns), F32)]
    return pl.pallas_call(
        near_kernel,
        in_specs=[SMEM, HBM] + [VMEM] * 4,
        out_specs=[VMEM] * len(outs),
        out_shape=outs,
        scratch_shapes=[
            pltpu.VMEM((3, g.shape[0], got.shape[0] // 3), BF16),
            pltpu.SemaphoreType.DMA((3 * PARTS,)),
        ],
        compiler_params=PARAMS,
        cost_estimate=SMALL,
        name="near_blocks",
    )(me, x, g, got, far_up, far_down)


def add_kernel(low, count, up, got_up, down, got_down, *rest):
    more, outs = rest[:count], rest[-2:]
    half = up.shape[0]
    for mine, got, out in ((up, got_up, outs[0]), (down, got_down, outs[1])):
        out[:half] = (mine[...] + got[pl.ds(low, half)].astype(F32)).astype(BF16)
    for value, out in zip(more, outs):
        out[half:] = value[...]


def add_far(low, up, got_up, down, got_down, more=(), earlier=()):
    rows = up.shape[0] + (more[0].shape[0] if more else 0)
    return pl.pallas_call(
        partial(add_kernel, low, len(more)),
        in_specs=[VMEM] * (4 + len(more)) + [HBM] * len(earlier),
        out_specs=[VMEM] * 2,
        out_shape=[shape(BF16, rows, up.shape[1])] * 2,
        compiler_params=PARAMS,
        cost_estimate=SMALL,
        name="add_far",
    )(up, got_up, down, got_down, *more, *earlier)


def fetch_kernel(places, *refs):
    count = len(places)
    copies = []
    for i, (start, rows) in enumerate(places):
        source, held, sems = refs[i], refs[count + i], refs[2 * count]
        part = rows // 2
        for k in range(2):
            copies.append(
                pltpu.make_async_copy(
                    source.at[pl.ds(start + k * part, part)], held.at[pl.ds(k * part, part)], sems.at[2 * i + k]
                )
            )
            copies[-1].start()
    for copy in copies:
        copy.wait()


def fetch(places, *arrays):
    return pl.pallas_call(
        partial(fetch_kernel, places),
        in_specs=[HBM] * len(arrays),
        out_specs=[VMEM] * len(arrays),
        out_shape=[shape(a.dtype, rows, a.shape[1]) for a, (_, rows) in zip(arrays, places)],
        scratch_shapes=[pltpu.SemaphoreType.DMA((2 * len(arrays),))],
        compiler_params=PARAMS,
        cost_estimate=SMALL,
        name="fetch",
    )(*arrays)


def step_kernel(first_row, places, step, push_weight, own, c_up, c_down, *refs):
    count = max(at for at, _, _ in places)
    b_ups, b_downs = (c_up, *refs[:count]), (c_down, *refs[count : 2 * count])
    master, one, two = refs[2 * count : 2 * count + 3]
    second_out, halfway_out, first_out, send, second_made, sems = refs[-6:]
    copies = []
    rows, columns = own.shape
    line = lax.broadcasted_iota(jnp.int32, (TAIL, columns), 0)
    left = jnp.full((TAIL, columns), push_weight[0], F32)
    high = left.astype(BF16).astype(F32)
    middle = (left - high).astype(BF16).astype(F32)
    low = left - high - middle
    parts = jnp.where(line == 0, high, jnp.where(line == 1, middle, jnp.where(line == 2, low, 0.0)))
    send[pl.ds(2 * rows, TAIL)] = parts.astype(BF16)
    half = rows // 2
    row = (1, columns)
    number = jnp.full(row, step[0] + 1, jnp.int32).astype(F32)
    scale_one = 1.0 / (1.0 - jnp.exp(number * math.log(BETA_ONE)))
    scale_two = 1.0 / (1.0 - jnp.exp(number * math.log(BETA_TWO)))
    decay = DECAY_RATE / jnp.full(row, push_weight[0], F32)
    for low, c, b_pieces in ((0, c_up, b_downs), (half, c_down, b_ups)):
        to = 0
        for which, b_low, size in places:
            at = pl.ds(low + to, size)
            far = b_pieces[which][pl.ds(b_low, size)].astype(F32)
            gradient = own[at] + (c[pl.ds(to, size)].astype(F32) + far)
            first = BETA_ONE * one[at] + (1.0 - BETA_ONE) * gradient
            second = BETA_TWO * two[at] + (1.0 - BETA_TWO) * gradient * gradient
            direction = first * scale_one / (jnp.sqrt(second * scale_two) + EPSILON)
            weights = master[at]
            halfway = weights - LEARN_RATE * (direction + weights * decay)
            second_made[at] = second
            halfway_out[at] = halfway
            first_out[at] = first
            send[at] = halfway.astype(BF16)
            send[pl.ds(rows + low + to, size)] = first.astype(BF16)
            to += size
        at = pl.ds(low, half)
        copies.append(
            pltpu.make_async_copy(second_made.at[at], second_out.at[pl.ds(first_row + low, half)], sems.at[len(copies)])
        )
        copies[-1].start()
    for copy in copies:
        copy.wait()


def step_chunk(first_row, height, places, ins, before=(), earlier=()):
    rows, columns = ins[2].shape
    return pl.pallas_call(
        partial(step_kernel, first_row, places),
        in_specs=[SMEM] * 2 + [VMEM] * (len(ins) - 2) + [HBM] * (len(before) + len(earlier)),
        out_specs=[HBM] + [VMEM] * 3,
        out_shape=[pltpu.HBM((height, columns), F32)]
        + [shape(F32, rows, columns)] * 2
        + [shape(BF16, 2 * rows + TAIL, columns)],
        scratch_shapes=[pltpu.VMEM((rows, columns), F32), pltpu.SemaphoreType.DMA((2,))],
        input_output_aliases={len(ins): 0} if before else {},
        compiler_params=PARAMS,
        cost_estimate=SMALL,
        name="step_chunk",
    )(*ins, *before, *earlier)


def mixed_scale(push_weight, tail):
    return 1.0 / (0.5 * (push_weight[0] + jnp.sum(tail.astype(F32), axis=0, keepdims=True)))


def mix_kernel(first_row, rows, push_weight, halfway, first, got, *rest):
    master_out, first_out, copy_out, master_new, first_new, copy, sems = rest[-7:]
    pieces = 2
    part = rows // pieces
    scale = mixed_scale(push_weight, got[pl.ds(2 * rows, TAIL)])
    sends = []
    for k in range(pieces):
        at, to = pl.ds(k * part, part), pl.ds(first_row + k * part, part)
        mixed = 0.5 * (halfway[at] + got[at].astype(F32))
        master_new[at] = mixed
        copy[at] = (mixed * scale).astype(BF16)
        first_new[at] = 0.5 * (first[at] + got[pl.ds(rows + k * part, part)].astype(F32))
        sends += [
            pltpu.make_async_copy(made.at[at], out.at[to], sems.at[3 * k + i])
            for i, (made, out) in enumerate(((master_new, master_out), (first_new, first_out), (copy, copy_out)))
        ]
        start(sends[3 * k :])
    wait(sends)


def mix_chunk(first_row, rows, height, push_weight, halfway, first, got, before=()):
    columns = halfway.shape[1]
    ins = (push_weight, halfway, first, got)
    return pl.pallas_call(
        partial(mix_kernel, first_row, rows),
        in_specs=[SMEM] + [VMEM] * 3 + [HBM] * len(before),
        out_specs=[HBM] * 3,
        out_shape=[pltpu.HBM((height, columns), F32)] * 2 + [pltpu.HBM((height, columns), BF16)],
        scratch_shapes=[
            pltpu.VMEM((rows, columns), F32),
            pltpu.VMEM((rows, columns), F32),
            pltpu.VMEM((rows, columns), BF16),
            pltpu.SemaphoreType.DMA((6,)),
        ],
        input_output_aliases={len(ins) + i: i for i in range(len(before))},
        compiler_params=PARAMS,
        cost_estimate=SMALL,
        name="mix_chunk",
    )(*ins, *before)


def pass_kernel(*refs):
    refs[-1][0] = jnp.int32(0)


def passed(*arrays):
    return pl.pallas_call(
        pass_kernel,
        in_specs=[HBM] * len(arrays),
        out_specs=[HBM] * len(arrays),
        out_shape=[pltpu.HBM(a.shape, a.dtype) for a in arrays],
        scratch_shapes=[pltpu.SMEM((1,), jnp.int32)],
        input_output_aliases={i: i for i in range(len(arrays))},
        compiler_params=PARAMS,
        cost_estimate=SMALL,
        name="passed",
    )(*arrays)


def up_z(block):
    count = lax.axis_size("fsdp")
    return lax.ppermute(block, "fsdp", [(i, (i + 2) % count) for i in range(count)])


def down_z(block):
    count = lax.axis_size("fsdp")
    return lax.ppermute(block, "fsdp", [(i, (i - 2) % count) for i in range(count)])


def other_core(block):
    return lax.ppermute(block, "fsdp", [(i, i ^ 1) for i in range(lax.axis_size("fsdp"))])


def from_partner(block, bit):
    return lax.ppermute(block, "rep", [(i, i ^ (1 << bit)) for i in range(lax.axis_size("rep"))])


def after(value, *earlier):
    return lax.optimization_barrier((value, *earlier))[0]


def exchanges(height, bit, push_weight, step_index, send_1, halfway_1, first_1, second, rest_up, rest_down, own_2, *state):
    (low_2, rows_2), half_2 = CHUNKS[1], CHUNKS[1][1] // 2
    got_1 = from_partner(send_1, bit)
    got_rest = up_z(rest_up), down_z(rest_down)
    *state_2, own_2 = fetch(((low_2, rows_2),) * 3 + ((0, rows_2),), *(in_hbm(v) for v in (*state, own_2)))
    second, halfway_2, first_2, send_2 = step_chunk(
        low_2,
        height,
        ((0, half_2, half_2),),
        (step_index, push_weight, own_2, *got_rest, *state_2),
        (second,),
    )
    got_2 = from_partner(send_2, bit)
    other_weight = from_partner(push_weight, bit)
    mixed = mix_chunk(*CHUNKS[0], height, push_weight, halfway_1, first_1, got_1)
    return (other_weight, second, *mix_chunk(*CHUNKS[1], height, push_weight, halfway_2, first_2, got_2, mixed))


def on_device(activations, cotangent, master, moment_one, moment_two, push_weight, step_index):
    x, g, state = in_hbm(activations), in_hbm(cotangent), [in_hbm(v[0]) for v in (master, moment_one, moment_two)]
    height = master.shape[1]
    bits = lax.axis_size("rep").bit_length() - 1

    me = jnp.full((1,), lax.axis_index("fsdp"), jnp.int32)
    (low_1, rows_1), (low_2, rows_2) = CHUNKS
    half_1, half_2 = rows_1 // 2, rows_2 // 2
    out_far, g_held = first_block(me, x, g, height)
    got_far = other_core(out_far)
    out_near, x_far = other_blocks(me, x, g_held, height)
    got_near = other_core(after(out_near, got_far))
    a_up_1, a_down_1, a_up_2, a_down_2 = far_block(x_far, g_held, got_far)
    got_a_up, got_a_down = up_z(a_up_1), down_z(a_down_1)
    b_up, b_down, *later, c_up_1, c_down_1, c_up_2, c_down_2, own_1, own_2 = near_blocks(
        me, x, g_held, got_near, a_up_2, a_down_2
    )
    got_b = up_z(b_up), down_z(b_down)
    state_1 = fetch([(low_1, rows_1)] * 3, *(after(v, b_up) for v in state))
    c_up_1, c_down_1 = add_far(0, c_up_1, got_a_up, c_down_1, got_a_down)
    got_c = up_z(c_up_1), down_z(c_down_1)
    rest = add_far(0, c_up_2, got_b[0], c_down_2, got_b[1], later, (*got_c, state_1[0]))
    second, *made_1 = step_chunk(
        low_1, height, ((1, half_2, half_1),), (step_index, push_weight, own_1, *got_c, *got_b, *state_1)
    )
    other_weight, *made = lax.switch(
        lax.rem(step_index[0], bits),
        [partial(exchanges, height, bit) for bit in range(bits)],
        push_weight,
        step_index,
        made_1[2],
        *made_1[:2],
        second,
        *rest,
        own_2,
        *state,
    )
    second, mixed, first, copy = passed(*made)
    weight_new = 0.5 * (push_weight + other_weight)
    return (mixed[None], first[None], second[None], weight_new, copy[None])


def solution(mesh):
    placed = (
        P(("rep", "fsdp"), None),
        P(("rep", "fsdp"), None),
        P("rep", "fsdp", None),
        P("rep", "fsdp", None),
        P("rep", "fsdp", None),
        P("rep"),
        P(),
    )
    return jax.shard_map(
        on_device,
        mesh=mesh,
        in_specs=placed,
        out_specs=(
            P("rep", "fsdp", None),
            P("rep", "fsdp", None),
            P("rep", "fsdp", None),
            P("rep"),
            P("rep", "fsdp", None),
        ),
        check_vma=False,
    )
```

```python
import math
from functools import partial

import jax
import jax.numpy as jnp
from jax import lax
from jax.experimental import pallas as pl
from jax.experimental.pallas import tpu as pltpu
from jax.sharding import PartitionSpec as P

BETA_ONE = 0.9
BETA_TWO = 0.95
LEARN_RATE = 0.01
DECAY_RATE = 0.1
EPSILON = 1e-08

F32 = jnp.float32
BF16 = jnp.bfloat16
HBM = pl.BlockSpec(memory_space=pltpu.HBM)
SMEM = pl.BlockSpec(memory_space=pltpu.SMEM)
VMEM = pl.BlockSpec(memory_space=pltpu.VMEM)
PARAMS = pltpu.CompilerParams(vmem_limit_bytes=16 * 1024 * 1024)
SMALL = pl.CostEstimate(flops=0, bytes_accessed=0, transcendentals=0)
CHUNKS = ((0, 320), (320, 192))
PARTS = 4
TAIL = 16


def shape(dtype, *sizes):
    return pltpu.VMEM(sizes, dtype)


def in_hbm(array):
    return pltpu.with_memory_space_constraint(array, pltpu.HBM)


def product(x, g):
    return lax.dot_general(x, g, (((0,), (0,)), ((), ())), preferred_element_type=F32)


def first_column(me, ahead, other, width, groups):
    group, core = lax.shift_right_logical(me[0], 1), lax.bitwise_and(me[0], 1)
    low = (2 * lax.rem(group + ahead % groups, groups) + (1 - core if other else core)) * width
    return pl.multiple_of(low, width)


def row_copies(source, columns, held, sems, first):
    part = source.shape[0] // PARTS
    return [
        pltpu.make_async_copy(source.at[pl.ds(i * part, part), columns], held.at[pl.ds(i * part, part)], sems.at[first + i])
        for i in range(PARTS)
    ]


def start(copies):
    for copy in copies:
        copy.start()


def wait(copies):
    for copy in copies:
        copy.wait()


def first_kernel(me, x, g, out, g_held, x_held, sems):
    width, columns = out.shape
    groups = x.shape[1] // (2 * width)
    g_copies = row_copies(g, pl.ds(0, columns), g_held, sems, 0)
    x_copies = row_copies(x, pl.ds(first_column(me, 2, True, width, groups), width), x_held, sems, PARTS)
    start(g_copies)
    start(x_copies)
    wait(g_copies)
    wait(x_copies)
    out[...] = product(x_held[...], g_held[...]).astype(BF16)


def first_block(me, x, g, width):
    tokens, columns = g.shape
    return pl.pallas_call(
        first_kernel,
        in_specs=[SMEM, HBM, HBM],
        out_specs=[VMEM] * 2,
        out_shape=[shape(BF16, width, columns), shape(BF16, tokens, columns)],
        scratch_shapes=[pltpu.VMEM((tokens, width), BF16), pltpu.SemaphoreType.DMA((2 * PARTS,))],
        compiler_params=PARAMS,
        cost_estimate=SMALL,
        name="first_block",
    )(me, x, g)


def column_blocks(me, x, other, held, sems, width):
    groups = x.shape[1] // (2 * width)
    return [
        row_copies(x, pl.ds(first_column(me, ahead, other, width, groups), width), held.at[k], sems, PARTS * k)
        for k, ahead in enumerate((1, -1, 0))
    ]


def others_kernel(me, x, g, out, far, x_held, sems):
    width = far.shape[1]
    groups = x.shape[1] // (2 * width)
    theirs = column_blocks(me, x, True, x_held, sems, width)
    own = row_copies(x, pl.ds(first_column(me, 2, False, width, groups), width), far, sems, 3 * PARTS)
    start(theirs[0])
    start(theirs[1])
    for k in range(3):
        wait(theirs[k])
        if k < 2:
            start((theirs[2], own)[k])
        out[pl.ds(k * width, width)] = product(x_held[k], g[...]).astype(BF16)
    wait(own)


def other_blocks(me, x, g, width):
    tokens, columns = g.shape
    return pl.pallas_call(
        others_kernel,
        in_specs=[SMEM, HBM, VMEM],
        out_specs=[VMEM] * 2,
        out_shape=[shape(BF16, 3 * width, columns), shape(BF16, tokens, width)],
        scratch_shapes=[pltpu.VMEM((3, tokens, width), BF16), pltpu.SemaphoreType.DMA((4 * PARTS,))],
        compiler_params=PARAMS,
        cost_estimate=SMALL,
        name="other_blocks",
    )(me, x, g)


def far_kernel(x, g, got, *outs):
    total = product(x[...], g[...]) + got[...].astype(F32)
    for k, (low, rows) in enumerate(CHUNKS):
        half = rows // 2
        outs[2 * k][...] = total[low : low + half].astype(BF16)
        outs[2 * k + 1][...] = total[low + half : low + rows].astype(BF16)


def far_block(x, g, got):
    columns = got.shape[1]
    return pl.pallas_call(
        far_kernel,
        in_specs=[VMEM] * 3,
        out_specs=[VMEM] * 4,
        out_shape=[shape(BF16, rows // 2, columns) for _, rows in CHUNKS for _ in range(2)],
        compiler_params=PARAMS,
        cost_estimate=SMALL,
        name="far_block",
    )(x, g, got)


def near_kernel(me, x, g, got, far_up, far_down, *outs):
    *outs, x_held, sems = outs
    b_up, b_down, rest_up, rest_down, c_up_1, c_down_1, c_up_2, c_down_2, own_1, own_2 = outs
    width = got.shape[0] // 3
    (low_1, rows_1), (low_2, rows_2) = CHUNKS
    half_1, half_2 = rows_1 // 2, rows_2 // 2

    blocks = column_blocks(me, x, False, x_held, sems, width)
    for copies in blocks:
        start(copies)

    def total(k):
        wait(blocks[k])
        return product(x_held[k], g[...]) + got[pl.ds(k * width, width)].astype(F32)

    def plain(values, chunk_1, chunk_2, far, b, rest):
        b[:half_2] = far[...]
        b[half_2:] = values[chunk_1 : chunk_1 + half_1].astype(BF16)
        rest[...] = values[chunk_2 : chunk_2 + half_2].astype(BF16)

    above = total(0)
    plain(above, low_1 + half_1, low_2 + half_2, far_up, b_up, rest_up)
    c_up_1[...] = above[low_1 : low_1 + half_1]
    c_up_2[...] = above[low_2 : low_2 + half_2]
    below = total(1)
    plain(below, low_1, low_2, far_down, b_down, rest_down)
    c_down_1[...] = below[low_1 + half_1 : low_1 + rows_1]
    c_down_2[...] = below[low_2 + half_2 : low_2 + rows_2]
    own = total(2)
    own_1[...] = own[low_1 : low_1 + rows_1]
    own_2[...] = own[low_2 : low_2 + rows_2]


def near_blocks(me, x, g, got, far_up, far_down):
    columns = g.shape[1]
    (_, rows_1), (_, rows_2) = CHUNKS
    half_1, half_2 = rows_1 // 2, rows_2 // 2
    outs = [shape(BF16, half_2 + half_1, columns)] * 2 + [shape(BF16, half_2, columns)] * 2
    outs += [shape(F32, half_1, columns)] * 2 + [shape(F32, half_2, columns)] * 2
    outs += [shape(F32, rows_1, columns), jax.ShapeDtypeStruct((rows_2, columns), F32)]
    return pl.pallas_call(
        near_kernel,
        in_specs=[SMEM, HBM] + [VMEM] * 4,
        out_specs=[VMEM] * len(outs),
        out_shape=outs,
        scratch_shapes=[
            pltpu.VMEM((3, g.shape[0], got.shape[0] // 3), BF16),
            pltpu.SemaphoreType.DMA((3 * PARTS,)),
        ],
        compiler_params=PARAMS,
        cost_estimate=SMALL,
        name="near_blocks",
    )(me, x, g, got, far_up, far_down)


def add_kernel(low, count, up, got_up, down, got_down, *rest):
    more, outs = rest[:count], rest[-2:]
    half = up.shape[0]
    for mine, got, out in ((up, got_up, outs[0]), (down, got_down, outs[1])):
        out[:half] = (mine[...] + got[pl.ds(low, half)].astype(F32)).astype(BF16)
    for value, out in zip(more, outs):
        out[half:] = value[...]


def add_far(low, up, got_up, down, got_down, more=(), earlier=()):
    rows = up.shape[0] + (more[0].shape[0] if more else 0)
    return pl.pallas_call(
        partial(add_kernel, low, len(more)),
        in_specs=[VMEM] * (4 + len(more)) + [HBM] * len(earlier),
        out_specs=[VMEM] * 2,
        out_shape=[shape(BF16, rows, up.shape[1])] * 2,
        compiler_params=PARAMS,
        cost_estimate=SMALL,
        name="add_far",
    )(up, got_up, down, got_down, *more, *earlier)


def fetch_kernel(places, *refs):
    count = len(places)
    copies = []
    for i, (start, rows) in enumerate(places):
        source, held, sems = refs[i], refs[count + i], refs[2 * count]
        part = rows // 2
        for k in range(2):
            copies.append(
                pltpu.make_async_copy(
                    source.at[pl.ds(start + k * part, part)], held.at[pl.ds(k * part, part)], sems.at[2 * i + k]
                )
            )
            copies[-1].start()
    for copy in copies:
        copy.wait()


def fetch(places, *arrays):
    return pl.pallas_call(
        partial(fetch_kernel, places),
        in_specs=[HBM] * len(arrays),
        out_specs=[VMEM] * len(arrays),
        out_shape=[shape(a.dtype, rows, a.shape[1]) for a, (_, rows) in zip(arrays, places)],
        scratch_shapes=[pltpu.SemaphoreType.DMA((2 * len(arrays),))],
        compiler_params=PARAMS,
        cost_estimate=SMALL,
        name="fetch",
    )(*arrays)


def step_kernel(first_row, places, step, push_weight, own, c_up, c_down, *refs):
    count = max(at for at, _, _ in places)
    b_ups, b_downs = (c_up, *refs[:count]), (c_down, *refs[count : 2 * count])
    master, one, two = refs[2 * count : 2 * count + 3]
    second_out, halfway_out, first_out, send, second_made, sems = refs[-6:]
    copies = []
    rows, columns = own.shape
    line = lax.broadcasted_iota(jnp.int32, (TAIL, columns), 0)
    left = jnp.full((TAIL, columns), push_weight[0], F32)
    high = left.astype(BF16).astype(F32)
    middle = (left - high).astype(BF16).astype(F32)
    low = left - high - middle
    parts = jnp.where(line == 0, high, jnp.where(line == 1, middle, jnp.where(line == 2, low, 0.0)))
    send[pl.ds(2 * rows, TAIL)] = parts.astype(BF16)
    half = rows // 2
    row = (1, columns)
    number = jnp.full(row, step[0] + 1, jnp.int32).astype(F32)
    scale_one = 1.0 / (1.0 - jnp.exp(number * math.log(BETA_ONE)))
    scale_two = 1.0 / (1.0 - jnp.exp(number * math.log(BETA_TWO)))
    decay = DECAY_RATE / jnp.full(row, push_weight[0], F32)
    for low, c, b_pieces in ((0, c_up, b_downs), (half, c_down, b_ups)):
        to = 0
        for which, b_low, size in places:
            at = pl.ds(low + to, size)
            far = b_pieces[which][pl.ds(b_low, size)].astype(F32)
            gradient = own[at] + (c[pl.ds(to, size)].astype(F32) + far)
            first = BETA_ONE * one[at] + (1.0 - BETA_ONE) * gradient
            second = BETA_TWO * two[at] + (1.0 - BETA_TWO) * gradient * gradient
            direction = first * scale_one / (jnp.sqrt(second * scale_two) + EPSILON)
            weights = master[at]
            halfway = weights - LEARN_RATE * (direction + weights * decay)
            second_made[at] = second
            halfway_out[at] = halfway
            first_out[at] = first
            send[at] = halfway.astype(BF16)
            send[pl.ds(rows + low + to, size)] = first.astype(BF16)
            to += size
        at = pl.ds(low, half)
        copies.append(
            pltpu.make_async_copy(second_made.at[at], second_out.at[pl.ds(first_row + low, half)], sems.at[len(copies)])
        )
        copies[-1].start()
    for copy in copies:
        copy.wait()


def step_chunk(first_row, height, places, ins, before=(), earlier=()):
    rows, columns = ins[2].shape
    return pl.pallas_call(
        partial(step_kernel, first_row, places),
        in_specs=[SMEM] * 2 + [VMEM] * (len(ins) - 2) + [HBM] * (len(before) + len(earlier)),
        out_specs=[HBM] + [VMEM] * 3,
        out_shape=[pltpu.HBM((height, columns), F32)]
        + [shape(F32, rows, columns)] * 2
        + [shape(BF16, 2 * rows + TAIL, columns)],
        scratch_shapes=[pltpu.VMEM((rows, columns), F32), pltpu.SemaphoreType.DMA((2,))],
        input_output_aliases={len(ins): 0} if before else {},
        compiler_params=PARAMS,
        cost_estimate=SMALL,
        name="step_chunk",
    )(*ins, *before, *earlier)


def mixed_scale(push_weight, tail):
    return 1.0 / (0.5 * (push_weight[0] + jnp.sum(tail.astype(F32), axis=0, keepdims=True)))


def mix_kernel(first_row, rows, push_weight, halfway, first, got, *rest):
    master_out, first_out, copy_out, master_new, first_new, copy, sems = rest[-7:]
    pieces = rows // 64
    part = rows // pieces
    scale = mixed_scale(push_weight, got[pl.ds(2 * rows, TAIL)])
    sends = []
    for k in range(pieces):
        at, to = pl.ds(k * part, part), pl.ds(first_row + k * part, part)
        mixed = 0.5 * (halfway[at] + got[at].astype(F32))
        master_new[at] = mixed
        copy[at] = (mixed * scale).astype(BF16)
        first_new[at] = 0.5 * (first[at] + got[pl.ds(rows + k * part, part)].astype(F32))
        sends += [
            pltpu.make_async_copy(made.at[at], out.at[to], sems.at[3 * k + i])
            for i, (made, out) in enumerate(((master_new, master_out), (first_new, first_out), (copy, copy_out)))
        ]
        start(sends[3 * k :])
    wait(sends)


def mix_chunk(first_row, rows, height, push_weight, halfway, first, got, before=()):
    columns = halfway.shape[1]
    ins = (push_weight, halfway, first, got)
    return pl.pallas_call(
        partial(mix_kernel, first_row, rows),
        in_specs=[SMEM] + [VMEM] * 3 + [HBM] * len(before),
        out_specs=[HBM] * 3,
        out_shape=[pltpu.HBM((height, columns), F32)] * 2 + [pltpu.HBM((height, columns), BF16)],
        scratch_shapes=[
            pltpu.VMEM((rows, columns), F32),
            pltpu.VMEM((rows, columns), F32),
            pltpu.VMEM((rows, columns), BF16),
            pltpu.SemaphoreType.DMA((3 * (rows // 64),)),
        ],
        input_output_aliases={len(ins) + i: i for i in range(len(before))},
        compiler_params=PARAMS,
        cost_estimate=SMALL,
        name="mix_chunk",
    )(*ins, *before)


def pass_kernel(*refs):
    refs[-1][0] = jnp.int32(0)


def passed(*arrays):
    return pl.pallas_call(
        pass_kernel,
        in_specs=[HBM] * len(arrays),
        out_specs=[HBM] * len(arrays),
        out_shape=[pltpu.HBM(a.shape, a.dtype) for a in arrays],
        scratch_shapes=[pltpu.SMEM((1,), jnp.int32)],
        input_output_aliases={i: i for i in range(len(arrays))},
        compiler_params=PARAMS,
        cost_estimate=SMALL,
        name="passed",
    )(*arrays)


def up_z(block):
    count = lax.axis_size("fsdp")
    return lax.ppermute(block, "fsdp", [(i, (i + 2) % count) for i in range(count)])


def down_z(block):
    count = lax.axis_size("fsdp")
    return lax.ppermute(block, "fsdp", [(i, (i - 2) % count) for i in range(count)])


def other_core(block):
    return lax.ppermute(block, "fsdp", [(i, i ^ 1) for i in range(lax.axis_size("fsdp"))])


def from_partner(block, bit):
    return lax.ppermute(block, "rep", [(i, i ^ (1 << bit)) for i in range(lax.axis_size("rep"))])


def after(value, *earlier):
    return lax.optimization_barrier((value, *earlier))[0]


def exchanges(height, bit, push_weight, step_index, send_1, halfway_1, first_1, second, rest_up, rest_down, own_2, *state):
    (low_2, rows_2), half_2 = CHUNKS[1], CHUNKS[1][1] // 2
    got_1 = from_partner(send_1, bit)
    got_rest = up_z(rest_up), down_z(rest_down)
    *state_2, own_2 = fetch(((low_2, rows_2),) * 3 + ((0, rows_2),), *(in_hbm(v) for v in (*state, own_2)))
    second, halfway_2, first_2, send_2 = step_chunk(
        low_2,
        height,
        ((0, half_2, half_2),),
        (step_index, push_weight, own_2, *got_rest, *state_2),
        (second,),
    )
    got_2 = from_partner(send_2, bit)
    other_weight = from_partner(push_weight, bit)
    mixed = mix_chunk(*CHUNKS[0], height, push_weight, halfway_1, first_1, got_1)
    return (other_weight, second, *mix_chunk(*CHUNKS[1], height, push_weight, halfway_2, first_2, got_2, mixed))


def on_device(activations, cotangent, master, moment_one, moment_two, push_weight, step_index):
    x, g, state = in_hbm(activations), in_hbm(cotangent), [in_hbm(v[0]) for v in (master, moment_one, moment_two)]
    height = master.shape[1]
    bits = lax.axis_size("rep").bit_length() - 1

    me = jnp.full((1,), lax.axis_index("fsdp"), jnp.int32)
    (low_1, rows_1), (low_2, rows_2) = CHUNKS
    half_1, half_2 = rows_1 // 2, rows_2 // 2
    out_far, g_held = first_block(me, x, g, height)
    got_far = other_core(out_far)
    out_near, x_far = other_blocks(me, x, g_held, height)
    got_near = other_core(after(out_near, got_far))
    a_up_1, a_down_1, a_up_2, a_down_2 = far_block(x_far, g_held, got_far)
    got_a_up, got_a_down = up_z(a_up_1), down_z(a_down_1)
    b_up, b_down, *later, c_up_1, c_down_1, c_up_2, c_down_2, own_1, own_2 = near_blocks(
        me, x, g_held, got_near, a_up_2, a_down_2
    )
    got_b = up_z(b_up), down_z(b_down)
    state_1 = fetch([(low_1, rows_1)] * 3, *(after(v, b_up) for v in state))
    c_up_1, c_down_1 = add_far(0, c_up_1, got_a_up, c_down_1, got_a_down)
    got_c = up_z(c_up_1), down_z(c_down_1)
    rest = add_far(0, c_up_2, got_b[0], c_down_2, got_b[1], later, (*got_c, state_1[0]))
    second, *made_1 = step_chunk(
        low_1, height, ((1, half_2, half_1),), (step_index, push_weight, own_1, *got_c, *got_b, *state_1)
    )
    other_weight, *made = lax.switch(
        lax.rem(step_index[0], bits),
        [partial(exchanges, height, bit) for bit in range(bits)],
        push_weight,
        step_index,
        made_1[2],
        *made_1[:2],
        second,
        *rest,
        own_2,
        *state,
    )
    second, mixed, first, copy = passed(*made)
    weight_new = 0.5 * (push_weight + other_weight)
    return (mixed[None], first[None], second[None], weight_new, copy[None])


def solution(mesh):
    placed = (
        P(("rep", "fsdp"), None),
        P(("rep", "fsdp"), None),
        P("rep", "fsdp", None),
        P("rep", "fsdp", None),
        P("rep", "fsdp", None),
        P("rep"),
        P(),
    )
    return jax.shard_map(
        on_device,
        mesh=mesh,
        in_specs=placed,
        out_specs=(
            P("rep", "fsdp", None),
            P("rep", "fsdp", None),
            P("rep", "fsdp", None),
            P("rep"),
            P("rep", "fsdp", None),
        ),
        check_vma=False,
    )
```
